32 devices in a mesh: blk: 16 (over z, y, x), rep: 2 (over core).
Axes of the slice: x: 2, y: 2, z: 4, core: 2. Of those that a mesh axis runs over, the one named last changes fastest.
Arguments:
- grad_out: bfloat16 [4096, 256], P(('blk', 'rep')), may hold values from -6 to 6
- preact: bfloat16 [4096, 256], P(('blk', 'rep')), may hold values from -6 to 6
- aggregated: bfloat16 [4096, 256], P(('blk', 'rep')), may hold values from -6 to 6
- weight: bfloat16 [256, 256], replicated, may hold values from -0.375 to 0.375
- degree: int32 [4096], P(('blk', 'rep')), may hold values from 4 to 64
- neighbors: int32 [16, 2, 16, 2, 8, 128], P('blk', 'rep'), may hold values from 0 to 127
- tile_col: int32 [16, 2, 16, 2], P('blk', 'rep'), may hold values from 0 to 1, as said below
- tile_count: int32 [16, 2, 16], P('blk', 'rep'), may hold values from 0 to 2, as said below
Outputs:
- grad_features: bfloat16 [4096, 256], P(('blk', 'rep'))
- grad_weight: float32 [256, 256], replicated
The draws below stay inside these ranges and needn't reach their ends.
Inputs may be any that keep to these rules, and one draw needn't show every extreme that they name: `tile_col`: the column tiles listed for one block, replica and source block are all different, also in slots at or past the count. `tile_count`: equal to 2 wherever the source block equals the block, and 0 wherever the source block is more than 2 blocks away from the block in both directions around the closed loop of 16 blocks.
All inputs are finite; a program needn't handle non-finite values.
Results may differ from the reference program's by a relative error of at most 0.0049.
Values may be sent and summed in bfloat16 or wider, within the bound.
A program may use at most 64 MiB of HBM per device.

```python
import jax
import jax.numpy as jnp
from jax import lax

HID = 256
TILE = 128
K = 8
REACH = 2
CAP = 2
NODES = 4096
N_BLK = 16
N_REP = 2


def draw_tile_col(key, part):
    scores = jax.random.randint(jax.random.fold_in(key, 11), (N_BLK, N_REP, N_BLK, N_REP), 0, 65536)
    ranked = scores * N_REP + jnp.arange(N_REP, dtype=jnp.int32)
    ordering = jnp.argsort(ranked, axis=-1)
    return ordering[..., :CAP].astype(jnp.int32)


def draw_tile_count(key, part):
    ceiling = jax.random.randint(jax.random.fold_in(key, 21), (N_BLK, N_REP, 1), 1, CAP + 1)
    drawn = jax.random.randint(jax.random.fold_in(key, 22), (N_BLK, N_REP, N_BLK), 0, 1048576)
    counts = drawn % ceiling + 1
    block_ids = jnp.arange(N_BLK, dtype=jnp.int32)[:, None, None]
    source_ids = jnp.arange(N_BLK, dtype=jnp.int32)[None, None, :]
    upward = (source_ids - block_ids) % N_BLK
    downward = (block_ids - source_ids) % N_BLK
    nearby = jnp.logical_or(upward <= REACH, downward <= REACH)
    diagonal = block_ids == source_ids
    banded = jnp.where(nearby, counts, 0)
    return jnp.where(diagonal, CAP, banded).astype(jnp.int32)


def place_ends(values, stream_key, least, largest):
    index_at = [jax.random.randint(jax.random.fold_in(stream_key, axis), (), 0, length) for axis, length in enumerate(values.shape)]
    longest = values.shape.index(max(values.shape))
    next_to = index_at[:longest] + [(index_at[longest] + 1) % values.shape[longest]] + index_at[longest + 1:]
    return values.at[tuple(index_at)].set(least).at[tuple(next_to)].set(largest)


def steps_of(own_key, dims, split, smallest, high):
    level, own = 1.0, jax.random.fold_in(own_key, 6)
    for dim, blocks in split:
        draws = jnp.exp(jax.random.uniform(jax.random.fold_in(own, dim), (blocks,), jnp.float32, smallest / len(split), high / len(split)))
        level = level * jnp.repeat(draws, dims[dim] // blocks).reshape([-1 if axis == dim else 1 for axis in range(len(dims))])
    return level


def centred(own_key, dims, spread, reach, pieces=(), held_as=jnp.bfloat16):
    entries = spread * jax.random.normal(own_key, dims, jnp.float32)
    if pieces:
        entries = entries * steps_of(own_key, dims, pieces, -0.22, 0.18)
    return jnp.clip(entries, -reach, reach).astype(held_as)


def setup_inputs(seed: int = 0) -> dict:
    splits = jax.random.split(jax.random.key(seed), 9)
    grad_out = centred(splits[0], (NODES, HID), 1.0, 6.0, ((0, 32),))
    preact = centred(splits[1], (NODES, HID), 1.0, 6.0, ((0, 32),))
    aggregated = centred(splits[2], (NODES, HID), 1.0, 6.0, ((0, 32),))
    weight = centred(splits[3], (HID, HID), HID ** -0.5, 0.375)
    degree = place_ends(jax.random.randint(splits[4], (NODES,), 4, 65), jax.random.fold_in(splits[4], 1), 4, 64).astype(jnp.int32)
    neighbors = place_ends(jax.random.randint(splits[5], (N_BLK, N_REP, N_BLK, CAP, K, TILE), 0, TILE), jax.random.fold_in(splits[5], 1), 0, TILE - 1).astype(jnp.int32)
    tile_col = draw_tile_col(jax.random.fold_in(splits[8], 71), 0)
    tile_count = draw_tile_count(jax.random.fold_in(splits[8], 71), 0)
    return dict(grad_out=grad_out, preact=preact, aggregated=aggregated, weight=weight, degree=degree, neighbors=neighbors, tile_col=tile_col, tile_count=tile_count)


def reference(grad_out, preact, aggregated, weight, degree, neighbors, tile_col, tile_count):
    grad_pre = jnp.where(preact > 0, grad_out, jnp.zeros_like(grad_out))
    raw_weight = lax.dot_general(aggregated, grad_pre, (((0,), (0,)), ((), ())), preferred_element_type=jnp.float32)
    norm_value = jnp.sqrt(jnp.sum(raw_weight * raw_weight) + 1e-06)
    grad_weight = raw_weight * jnp.minimum(1.0, 128.0 / norm_value)
    inv_root = 1.0 / jnp.sqrt(degree.astype(jnp.float32))
    backward = lax.dot_general(grad_pre, weight, (((1,), (1,)), ((), ())), preferred_element_type=jnp.float32)
    scaled = (backward * inv_root[:, None]).astype(jnp.bfloat16)
    blocks_rows = scaled.reshape(N_BLK, N_REP, TILE, HID)
    positions = jnp.arange(TILE, dtype=jnp.int32)
    slot_index = jnp.arange(CAP, dtype=jnp.int32)
    replicas = jnp.arange(N_REP, dtype=jnp.int32)

    def one_device(block, replica):
        listed = neighbors[block, replica]
        adjacency = lax.optimization_barrier(jnp.sum((listed[:, :, :, None, :] == positions[None, None, None, :, None]).astype(jnp.float32), axis=2))
        present = (slot_index[None, :] < tile_count[block, replica][:, None]).astype(jnp.float32)
        adjacency = adjacency * present[:, :, None, None]
        row_data = lax.dynamic_index_in_dim(blocks_rows, replica, 1, keepdims=False).astype(jnp.float32)
        contribution = jnp.einsum('tsci,tif->tscf', adjacency, row_data)
        chooser = (tile_col[block, replica][:, :, None] == replicas[None, None, :]).astype(jnp.float32)
        return jnp.einsum('tsn,tscf->ncf', chooser, contribution)

    def one_block(block):

        def for_replica(replica):
            return one_device(block, replica)
        return lax.optimization_barrier(jnp.sum(lax.map(for_replica, replicas), axis=0))
    propagated = lax.map(one_block, jnp.arange(N_BLK, dtype=jnp.int32))
    propagated = propagated.reshape(NODES, HID)
    grad_features = (propagated * inv_root[:, None]).astype(jnp.bfloat16)
    return (grad_features, grad_weight)
```

```python
import functools

import jax
import jax.numpy as jnp
from jax import lax
from jax.experimental import pallas as pl
from jax.experimental.pallas import tpu as pltpu
from jax.sharding import PartitionSpec as P

MESH = pl.DeviceIdType.MESH
REACH = 2
LANES = 128
PACKED_ROWS = 16


def kernel(
    blocks,
    replicas,
    members,
    offsets,
    grad_out_hbm,
    preact_hbm,
    aggregated_hbm,
    weight_hbm,
    degree_ref,
    neighbors_hbm,
    column_ref,
    count_ref,
    features_ref,
    weight_out_ref,
    grad_out_ref,
    preact_ref,
    aggregated_ref,
    weight_ref,
    listed_ref,
    local_ref,
    part_ref,
    spread_ref,
    across_ref,
    gathered_ref,
    rows_ref,
    tiles_ref,
    partial_ref,
    landed_ref,
    load_sem,
    spread_sem,
    across_sem,
    gather_sem,
    rows_send_sem,
    rows_recv_sem,
    partial_send_sem,
    partial_recv_sem,
):
    block, replica = lax.axis_index("blk"), lax.axis_index("rep")
    me = block * replicas + replica
    groups = blocks * replicas // members
    group, member = me // members, lax.rem(me, members)
    tile_side, hidden = grad_out_ref.shape
    slots = listed_ref.shape[1]
    depth = listed_ref.shape[2]
    piece = part_ref.shape[0] // members
    halves = hidden // LANES

    def device(flat):
        return (flat // replicas, lax.rem(flat, replicas))

    def group_peer(step):
        return group * members + lax.rem(member + step, members)

    def across_peer(step):
        return lax.rem(group + step, groups) * members + member

    def near_device(offset):
        return (lax.rem(block + offset + blocks, blocks), replica)

    def replica_device(step):
        return (block, lax.rem(replica + step, replicas))

    def piece_rows(index):
        return pl.ds(pl.multiple_of(index * piece, piece), piece)

    barrier = pltpu.get_barrier_semaphore()

    def greet(target):
        pl.semaphore_signal(barrier, inc=1, device_id=target, device_id_type=MESH)

    def greet_member(step, carry):
        greet(device(group_peer(step)))
        return carry

    lax.fori_loop(1, members, greet_member, 0)
    greeted = members - 1
    if groups > 1:
        for step in range(1, groups):
            greet(device(across_peer(step)))
        for offset in offsets:
            greet(near_device(offset))
        for step in range(1, replicas):
            greet(replica_device(step))
        greeted += groups - 1 + len(offsets) + replicas - 1

    loads = [
        pltpu.make_async_copy(source, target, load_sem.at[index])
        for index, (source, target) in enumerate(
            (
                (grad_out_hbm, grad_out_ref),
                (preact_hbm, preact_ref),
                (aggregated_hbm, aggregated_ref),
                (weight_hbm, weight_ref),
            )
        )
    ]
    sources = [block] + [lax.rem(block - offset + blocks, blocks) for offset in offsets]
    for index, source in enumerate(sources):
        loads.append(
            pltpu.make_async_copy(
                neighbors_hbm.at[0, 0, source], listed_ref.at[index], load_sem.at[4 + index]
            )
        )
    for load in loads:
        load.start()

    inverse = 1.0 / jnp.sqrt(degree_ref[...].astype(jnp.float32))
    inverse = jnp.transpose(jnp.broadcast_to(inverse, (tile_side, tile_side)))[:, :1]

    loads[0].wait()
    loads[1].wait()
    loads[2].wait()
    grad_pre = jnp.where(
        preact_ref[...].astype(jnp.float32) > 0, grad_out_ref[...].astype(jnp.float32), 0.0
    ).astype(jnp.bfloat16)
    local = lax.dot_general(
        aggregated_ref[...], grad_pre, (((0,), (0,)), ((), ())), preferred_element_type=jnp.float32
    )
    for half in range(halves):
        rows = pl.ds(half * hidden, hidden)
        columns = local[:, half * LANES : (half + 1) * LANES]
        local_ref[rows] = columns
        part_ref[rows] = columns.astype(jnp.bfloat16)
    loads[3].wait()
    backward = lax.dot_general(
        grad_pre, weight_ref[...], (((1,), (1,)), ((), ())), preferred_element_type=jnp.float32
    )
    rows_ref[pl.ds(0, tile_side)] = (backward * inverse).astype(jnp.bfloat16)

    pl.semaphore_wait(barrier, greeted)

    def send_piece(step, carry):
        peer = group_peer(step)
        pltpu.make_async_remote_copy(
            src_ref=part_ref.at[piece_rows(lax.rem(peer, members))],
            dst_ref=spread_ref.at[piece_rows(step - 1)],
            send_sem=spread_sem.at[0],
            recv_sem=spread_sem.at[1],
            device_id=device(peer),
            device_id_type=MESH,
        ).start()
        return carry

    lax.fori_loop(1, members, send_piece, 0)

    row_copies = []
    for index, offset in enumerate(offsets):
        copy = pltpu.make_async_remote_copy(
            src_ref=rows_ref.at[pl.ds(0, tile_side)],
            dst_ref=rows_ref.at[pl.ds((index + 1) * tile_side, tile_side)],
            send_sem=rows_send_sem.at[index],
            recv_sem=rows_recv_sem.at[index],
            device_id=near_device(offset),
            device_id_type=MESH,
        )
        copy.start()
        row_copies.append(copy)

    positions = lax.broadcasted_iota(jnp.int32, (tile_side, tile_side), 0)
    for index, source in enumerate(sources):
        loads[4 + index].wait()
        totals = [jnp.zeros((tile_side, tile_side), jnp.float32) for _ in range(replicas)]
        for slot in range(slots):
            counted = jnp.zeros((tile_side, tile_side), jnp.float32)
            for entry in range(depth):
                listed = listed_ref[index, slot, pl.ds(entry, 1), :]
                counted += jnp.where(listed == positions, 1.0, 0.0)
            column = column_ref[0, 0, slot, source]
            present = slot < count_ref[0, 0, source]
            for step in range(replicas):
                here = jnp.logical_and(present, column == lax.rem(replica + step, replicas))
                totals[step] += counted * jnp.where(here, 1.0, 0.0)
        for step in range(replicas):
            tiles_ref[
                pl.ds(step * tile_side, tile_side), pl.ds(index * tile_side, tile_side)
            ] = totals[step].astype(jnp.bfloat16)

    def product(first_row, row_count, first_source, source_count):
        return jnp.dot(
            tiles_ref[
                pl.ds(first_row * tile_side, row_count * tile_side),
                pl.ds(first_source * tile_side, source_count * tile_side),
            ],
            rows_ref[pl.ds(first_source * tile_side, source_count * tile_side)],
            preferred_element_type=jnp.float32,
        )

    def wait_all(ref, sem, count):
        rows = ref.at[pl.ds(0, count * piece)]
        pltpu.make_async_copy(rows, rows, sem).wait()

    wait_all(spread_ref, spread_sem.at[1], members - 1)
    reduced = local_ref[piece_rows(member)]
    for step in range(members - 1):
        reduced += spread_ref[pl.ds(step * piece, piece)].astype(jnp.float32)

    if groups > 1:
        across_ref[0] = reduced
        across_copies = []
        for step in range(1, groups):
            copy = pltpu.make_async_remote_copy(
                src_ref=across_ref.at[0],
                dst_ref=across_ref.at[step],
                send_sem=across_sem.at[0, step],
                recv_sem=across_sem.at[1, step],
                device_id=device(across_peer(step)),
                device_id_type=MESH,
            )
            copy.start()
            across_copies.append(copy)
        for step in range(1, groups):
            across_copies[step - 1].wait()
            reduced += across_ref[step]

    gathered_ref[piece_rows(member)] = reduced.astype(jnp.bfloat16)

    def send_reduced(step, carry):
        pltpu.make_async_remote_copy(
            src_ref=gathered_ref.at[piece_rows(member)],
            dst_ref=gathered_ref.at[piece_rows(member)],
            send_sem=gather_sem.at[0],
            recv_sem=gather_sem.at[1],
            device_id=device(group_peer(step)),
            device_id_type=MESH,
        ).start()
        return carry

    lax.fori_loop(1, members, send_reduced, 0)

    for copy in row_copies:
        copy.wait_recv()
    partial_copies = []
    if replicas > 1:
        partial_ref[...] = product(1, replicas - 1, 0, len(sources))
        for step in range(1, replicas):
            copy = pltpu.make_async_remote_copy(
                src_ref=partial_ref.at[pl.ds((step - 1) * tile_side, tile_side)],
                dst_ref=landed_ref.at[pl.ds((step - 1) * tile_side, tile_side)],
                send_sem=partial_send_sem.at[step - 1],
                recv_sem=partial_recv_sem.at[step - 1],
                device_id=replica_device(step),
                device_id_type=MESH,
            )
            copy.start()
            partial_copies.append(copy)
    owned = product(0, 1, 0, len(sources))
    for step, copy in enumerate(partial_copies):
        copy.wait_recv()
        owned += landed_ref[pl.ds(step * tile_side, tile_side)]
    features_ref[...] = (owned * inverse).astype(jnp.bfloat16)

    wait_all(gathered_ref, gather_sem.at[1], members - 1)
    raw = gathered_ref[...].astype(jnp.float32)
    total = jnp.sum(jnp.sum(raw * raw, axis=0, keepdims=True), axis=1, keepdims=True)
    scale = jnp.minimum(1.0, 128.0 / jnp.sqrt(total + 1e-06))
    for half in range(halves):
        weight_out_ref[:, pl.ds(half * LANES, LANES)] = (
            raw[half * hidden : (half + 1) * hidden] * scale
        )

    wait_all(spread_ref, spread_sem.at[0], members - 1)
    wait_all(gathered_ref, gather_sem.at[0], members - 1)
    for copy in row_copies + partial_copies:
        copy.wait_send()


def on_device(
    blocks, replicas, grad_out, preact, aggregated, weight, degree, neighbors, tile_col, tile_count
):
    tile_side, hidden = grad_out.shape
    slots, depth = neighbors.shape[3], neighbors.shape[4]
    packed = hidden * hidden // LANES
    members = min(blocks * replicas, packed // PACKED_ROWS)
    groups = blocks * replicas // members
    piece = packed // members
    offsets = []
    for distance in range(1, REACH + 1):
        for offset in (distance, -distance):
            if offset % blocks and offset % blocks not in [o % blocks for o in offsets]:
                offsets.append(offset)
    near = len(offsets) + 1
    others = max(replicas - 1, 1)
    hbm = pl.BlockSpec(memory_space=pltpu.HBM)
    vmem = pl.BlockSpec(memory_space=pltpu.VMEM)
    smem = pl.BlockSpec(memory_space=pltpu.SMEM)
    return pl.pallas_call(
        functools.partial(kernel, blocks, replicas, members, tuple(offsets)),
        out_shape=(
            jax.ShapeDtypeStruct((tile_side, hidden), jnp.bfloat16),
            jax.ShapeDtypeStruct((hidden, hidden), jnp.float32),
        ),
        in_specs=[hbm, hbm, hbm, hbm, vmem, hbm, smem, smem],
        out_specs=(vmem, vmem),
        scratch_shapes=[
            pltpu.VMEM((tile_side, hidden), jnp.bfloat16),
            pltpu.VMEM((tile_side, hidden), jnp.bfloat16),
            pltpu.VMEM((tile_side, hidden), jnp.bfloat16),
            pltpu.VMEM((hidden, hidden), jnp.bfloat16),
            pltpu.VMEM((near, slots, depth, tile_side), jnp.int32),
            pltpu.VMEM((packed, LANES), jnp.float32),
            pltpu.VMEM((packed, LANES), jnp.bfloat16),
            pltpu.VMEM((packed, LANES), jnp.bfloat16),
            pltpu.VMEM((groups, piece, LANES), jnp.float32),
            pltpu.VMEM((packed, LANES), jnp.bfloat16),
            pltpu.VMEM((near * tile_side, hidden), jnp.bfloat16),
            pltpu.VMEM((replicas * tile_side, near * tile_side), jnp.bfloat16),
            pltpu.VMEM((others * tile_side, hidden), jnp.float32),
            pltpu.VMEM((others * tile_side, hidden), jnp.float32),
            pltpu.SemaphoreType.DMA((4 + near,)),
            pltpu.SemaphoreType.DMA((2,)),
            pltpu.SemaphoreType.DMA((2, groups)),
            pltpu.SemaphoreType.DMA((2,)),
            pltpu.SemaphoreType.DMA((near,)),
            pltpu.SemaphoreType.DMA((near,)),
            pltpu.SemaphoreType.DMA((others,)),
            pltpu.SemaphoreType.DMA((others,)),
        ],
        compiler_params=pltpu.CompilerParams(
            collective_id=0, has_side_effects=True, vmem_limit_bytes=32 * 1024 * 1024
        ),
    )(
        grad_out,
        preact,
        aggregated,
        weight,
        degree.reshape(1, tile_side),
        neighbors,
        jnp.swapaxes(tile_col, 2, 3),
        tile_count,
    )


def solution(mesh):
    return jax.shard_map(
        functools.partial(on_device, mesh.shape["blk"], mesh.shape["rep"]),
        mesh=mesh,
        in_specs=(
            P(("blk", "rep"), None),
            P(("blk", "rep"), None),
            P(("blk", "rep"), None),
            P(),
            P(("blk", "rep")),
            P("blk", "rep", None, None, None, None),
            P("blk", "rep", None, None),
            P("blk", "rep", None),
        ),
        out_specs=(P(("blk", "rep"), None), P()),
        check_vma=False,
    )
```

```python
import functools

import jax
import jax.numpy as jnp
from jax import lax
from jax.experimental import pallas as pl
from jax.experimental.pallas import tpu as pltpu
from jax.sharding import PartitionSpec as P

MESH = pl.DeviceIdType.MESH
REACH = 2
LANES = 128
PACKED_ROWS = 16


def kernel(
    blocks,
    replicas,
    members,
    offsets,
    grad_out_hbm,
    preact_hbm,
    aggregated_hbm,
    weight_hbm,
    degree_ref,
    neighbors_hbm,
    column_ref,
    count_ref,
    features_ref,
    weight_out_ref,
    grad_out_ref,
    preact_ref,
    aggregated_ref,
    weight_ref,
    listed_ref,
    local_ref,
    part_ref,
    spread_ref,
    across_ref,
    gathered_ref,
    rows_ref,
    tiles_ref,
    partial_ref,
    landed_ref,
    load_sem,
    spread_sem,
    across_sem,
    gather_sem,
    rows_send_sem,
    rows_recv_sem,
    partial_send_sem,
    partial_recv_sem,
):
    block, replica = lax.axis_index("blk"), lax.axis_index("rep")
    me = block * replicas + replica
    groups = blocks * replicas // members
    group, member = me // members, lax.rem(me, members)
    tile_side, hidden = grad_out_ref.shape
    slots = listed_ref.shape[1]
    depth = listed_ref.shape[2]
    piece = part_ref.shape[0] // members
    halves = hidden // LANES

    def device(flat):
        return (flat // replicas, lax.rem(flat, replicas))

    def group_peer(step):
        return group * members + lax.rem(member + step, members)

    def across_peer(step):
        return lax.rem(group + step, groups) * members + member

    def near_device(offset):
        return (lax.rem(block + offset + blocks, blocks), replica)

    def replica_device(step):
        return (block, lax.rem(replica + step, replicas))

    def piece_rows(index):
        return pl.ds(pl.multiple_of(index * piece, piece), piece)

    barrier = pltpu.get_barrier_semaphore()

    def greet(target):
        pl.semaphore_signal(barrier, inc=1, device_id=target, device_id_type=MESH)

    def greet_member(step, carry):
        greet(device(group_peer(step)))
        return carry

    lax.fori_loop(1, members, greet_member, 0)
    greeted = members - 1
    if groups > 1:
        for step in range(1, groups):
            greet(device(across_peer(step)))
        for offset in offsets:
            greet(near_device(offset))
        for step in range(1, replicas):
            greet(replica_device(step))
        greeted += groups - 1 + len(offsets) + replicas - 1

    loads = [
        pltpu.make_async_copy(source, target, load_sem.at[index])
        for index, (source, target) in enumerate(
            (
                (grad_out_hbm, grad_out_ref),
                (preact_hbm, preact_ref),
                (aggregated_hbm, aggregated_ref),
                (weight_hbm, weight_ref),
            )
        )
    ]
    sources = [block] + [lax.rem(block - offset + blocks, blocks) for offset in offsets]
    for index, source in enumerate(sources):
        loads.append(
            pltpu.make_async_copy(
                neighbors_hbm.at[0, 0, source], listed_ref.at[index], load_sem.at[4 + index]
            )
        )
    for load in loads:
        load.start()

    inverse = 1.0 / jnp.sqrt(degree_ref[...].astype(jnp.float32))
    inverse = jnp.transpose(jnp.broadcast_to(inverse, (tile_side, tile_side)))[:, :1]

    loads[0].wait()
    loads[1].wait()
    loads[2].wait()
    grad_pre = jnp.where(
        preact_ref[...].astype(jnp.float32) > 0, grad_out_ref[...].astype(jnp.float32), 0.0
    ).astype(jnp.bfloat16)
    local = lax.dot_general(
        aggregated_ref[...], grad_pre, (((0,), (0,)), ((), ())), preferred_element_type=jnp.float32
    )
    for half in range(halves):
        rows = pl.ds(half * hidden, hidden)
        columns = local[:, half * LANES : (half + 1) * LANES]
        local_ref[rows] = columns
        part_ref[rows] = columns.astype(jnp.bfloat16)
    loads[3].wait()
    backward = lax.dot_general(
        grad_pre, weight_ref[...], (((1,), (1,)), ((), ())), preferred_element_type=jnp.float32
    )
    rows_ref[pl.ds(0, tile_side)] = (backward * inverse).astype(jnp.bfloat16)

    pl.semaphore_wait(barrier, greeted)

    def send_piece(step, carry):
        peer = group_peer(step)
        pltpu.make_async_remote_copy(
            src_ref=part_ref.at[piece_rows(lax.rem(peer, members))],
            dst_ref=spread_ref.at[piece_rows(step - 1)],
            send_sem=spread_sem.at[0],
            recv_sem=spread_sem.at[1],
            device_id=device(peer),
            device_id_type=MESH,
        ).start()
        return carry

    lax.fori_loop(1, members, send_piece, 0)

    row_copies = []
    for index, offset in enumerate(offsets):
        copy = pltpu.make_async_remote_copy(
            src_ref=rows_ref.at[pl.ds(0, tile_side)],
            dst_ref=rows_ref.at[pl.ds((index + 1) * tile_side, tile_side)],
            send_sem=rows_send_sem.at[index],
            recv_sem=rows_recv_sem.at[index],
            device_id=near_device(offset),
            device_id_type=MESH,
        )
        copy.start()
        row_copies.append(copy)

    positions = lax.broadcasted_iota(jnp.int32, (tile_side, tile_side), 0)
    for index, source in enumerate(sources):
        loads[4 + index].wait()
        totals = [jnp.zeros((tile_side, tile_side), jnp.float32) for _ in range(replicas)]
        for slot in range(slots):
            counted = jnp.zeros((tile_side, tile_side), jnp.float32)
            for entry in range(depth):
                listed = listed_ref[index, slot, pl.ds(entry, 1), :]
                counted += jnp.where(listed == positions, 1.0, 0.0)
            column = column_ref[0, 0, slot, source]
            present = slot < count_ref[0, 0, source]
            for step in range(replicas):
                here = jnp.logical_and(present, column == lax.rem(replica + step, replicas))
                totals[step] += counted * jnp.where(here, 1.0, 0.0)
        for step in range(replicas):
            tiles_ref[
                pl.ds(step * tile_side, tile_side), pl.ds(index * tile_side, tile_side)
            ] = totals[step].astype(jnp.bfloat16)

    def product(first_row, row_count, first_source, source_count):
        return jnp.dot(
            tiles_ref[
                pl.ds(first_row * tile_side, row_count * tile_side),
                pl.ds(first_source * tile_side, source_count * tile_side),
            ],
            rows_ref[pl.ds(first_source * tile_side, source_count * tile_side)],
            preferred_element_type=jnp.float32,
        )

    def wait_all(ref, sem, count):
        rows = ref.at[pl.ds(0, count * piece)]
        pltpu.make_async_copy(rows, rows, sem).wait()

    wait_all(spread_ref, spread_sem.at[1], members - 1)
    reduced = local_ref[piece_rows(member)]
    for step in range(members - 1):
        reduced += spread_ref[pl.ds(step * piece, piece)].astype(jnp.float32)

    if groups > 1:
        across_ref[0] = reduced
        across_copies = []
        for step in range(1, groups):
            copy = pltpu.make_async_remote_copy(
                src_ref=across_ref.at[0],
                dst_ref=across_ref.at[step],
                send_sem=across_sem.at[0, step],
                recv_sem=across_sem.at[1, step],
                device_id=device(across_peer(step)),
                device_id_type=MESH,
            )
            copy.start()
            across_copies.append(copy)
        for step in range(1, groups):
            across_copies[step - 1].wait()
            reduced += across_ref[step]

    gathered_ref[piece_rows(member)] = reduced.astype(jnp.bfloat16)

    def send_reduced(step, carry):
        pltpu.make_async_remote_copy(
            src_ref=gathered_ref.at[piece_rows(member)],
            dst_ref=gathered_ref.at[piece_rows(member)],
            send_sem=gather_sem.at[0],
            recv_sem=gather_sem.at[1],
            device_id=device(group_peer(step)),
            device_id_type=MESH,
        ).start()
        return carry

    lax.fori_loop(1, members, send_reduced, 0)

    for copy in row_copies:
        copy.wait_recv()
    partial_copies = []
    if replicas > 1:
        partial_ref[...] = product(1, replicas - 1, 0, len(sources))
        for step in range(1, replicas):
            copy = pltpu.make_async_remote_copy(
                src_ref=partial_ref.at[pl.ds((step - 1) * tile_side, tile_side)],
                dst_ref=landed_ref.at[pl.ds((step - 1) * tile_side, tile_side)],
                send_sem=partial_send_sem.at[step - 1],
                recv_sem=partial_recv_sem.at[step - 1],
                device_id=replica_device(step),
                device_id_type=MESH,
            )
            copy.start()
            partial_copies.append(copy)
    owned = product(0, 1, 0, len(sources))
    for step, copy in enumerate(partial_copies):
        copy.wait_recv()
        owned += landed_ref[pl.ds(step * tile_side, tile_side)]
    features_ref[...] = (owned * inverse).astype(jnp.bfloat16)

    wait_all(gathered_ref, gather_sem.at[1], members - 1)
    raw = gathered_ref[...].astype(jnp.float32)
    total = jnp.sum(jnp.sum(raw * raw, axis=0, keepdims=True), axis=1, keepdims=True)
    scale = jnp.minimum(1.0, 128.0 / jnp.sqrt(total + 1e-06))
    for half in range(halves):
        weight_out_ref[:, pl.ds(half * LANES, LANES)] = (
            raw[half * hidden : (half + 1) * hidden] * scale
        )

    wait_all(spread_ref, spread_sem.at[0], members - 1)
    wait_all(gathered_ref, gather_sem.at[0], members - 1)
    for copy in row_copies + partial_copies:
        copy.wait_send()


def on_device(
    blocks, replicas, grad_out, preact, aggregated, weight, degree, neighbors, tile_col, tile_count
):
    tile_side, hidden = grad_out.shape
    slots, depth = neighbors.shape[3], neighbors.shape[4]
    packed = hidden * hidden // LANES
    members = min(blocks * replicas, packed // PACKED_ROWS)
    groups = blocks * replicas // members
    piece = packed // members
    offsets = []
    for distance in range(1, REACH + 1):
        for offset in (distance, -distance):
            if offset % blocks and offset % blocks not in [o % blocks for o in offsets]:
                offsets.append(offset)
    near = len(offsets) + 1
    others = max(replicas - 1, 1)
    hbm = pl.BlockSpec(memory_space=pltpu.HBM)
    vmem = pl.BlockSpec(memory_space=pltpu.VMEM)
    smem = pl.BlockSpec(memory_space=pltpu.SMEM)
    return pl.pallas_call(
        functools.partial(kernel, blocks, replicas, members, tuple(offsets)),
        out_shape=(
            jax.ShapeDtypeStruct((tile_side, hidden), jnp.bfloat16),
            jax.ShapeDtypeStruct((hidden, hidden), jnp.float32),
        ),
        in_specs=[hbm, hbm, hbm, hbm, vmem, hbm, smem, smem],
        out_specs=(vmem, vmem),
        scratch_shapes=[
            pltpu.VMEM((tile_side, hidden), jnp.bfloat16),
            pltpu.VMEM((tile_side, hidden), jnp.bfloat16),
            pltpu.VMEM((tile_side, hidden), jnp.bfloat16),
            pltpu.VMEM((hidden, hidden), jnp.bfloat16),
            pltpu.VMEM((near, slots, depth, tile_side), jnp.int32),
            pltpu.VMEM((packed, LANES), jnp.float32),
            pltpu.VMEM((packed, LANES), jnp.bfloat16),
            pltpu.VMEM((packed, LANES), jnp.bfloat16),
            pltpu.VMEM((groups, piece, LANES), jnp.float32),
            pltpu.VMEM((packed, LANES), jnp.bfloat16),
            pltpu.VMEM((near * tile_side, hidden), jnp.bfloat16),
            pltpu.VMEM((replicas * tile_side, near * tile_side), jnp.bfloat16),
            pltpu.VMEM((others * tile_side, hidden), jnp.float32),
            pltpu.VMEM((others * tile_side, hidden), jnp.float32),
            pltpu.SemaphoreType.DMA((4 + near,)),
            pltpu.SemaphoreType.DMA((2,)),
            pltpu.SemaphoreType.DMA((2, groups)),
            pltpu.SemaphoreType.DMA((2,)),
            pltpu.SemaphoreType.DMA((near,)),
            pltpu.SemaphoreType.DMA((near,)),
            pltpu.SemaphoreType.DMA((others,)),
            pltpu.SemaphoreType.DMA((others,)),
        ],
        compiler_params=pltpu.CompilerParams(
            collective_id=0, has_side_effects=True, vmem_limit_bytes=63 * 1024 * 1024
        ),
    )(
        grad_out,
        preact,
        aggregated,
        weight,
        degree.reshape(1, tile_side),
        neighbors,
        jnp.swapaxes(tile_col, 2, 3),
        tile_count,
    )


def solution(mesh):
    return jax.shard_map(
        functools.partial(on_device, mesh.shape["blk"], mesh.shape["rep"]),
        mesh=mesh,
        in_specs=(
            P(("blk", "rep"), None),
            P(("blk", "rep"), None),
            P(("blk", "rep"), None),
            P(),
            P(("blk", "rep")),
            P("blk", "rep", None, None, None, None),
            P("blk", "rep", None, None),
            P("blk", "rep", None),
        ),
        out_specs=(P(("blk", "rep"), None), P()),
        check_vma=False,
    )
```

```python
import functools

import jax
import jax.numpy as jnp
from jax import lax
from jax.experimental import pallas as pl
from jax.experimental.pallas import tpu as pltpu
from jax.sharding import PartitionSpec as P

MESH = pl.DeviceIdType.MESH
REACH = 2
LANES = 128
PACKED_ROWS = 16


def kernel(
    blocks,
    replicas,
    members,
    offsets,
    grad_out_hbm,
    preact_hbm,
    aggregated_hbm,
    weight_hbm,
    degree_ref,
    neighbors_hbm,
    column_ref,
    count_ref,
    features_ref,
    weight_out_ref,
    grad_out_ref,
    preact_ref,
    aggregated_ref,
    weight_ref,
    listed_ref,
    local_ref,
    shared_ref,
    mine_ref,
    part_ref,
    spread_ref,
    across_ref,
    gathered_ref,
    rows_ref,
    tiles_ref,
    partial_ref,
    landed_ref,
    load_sem,
    shared_send_sem,
    shared_recv_sem,
    spread_sem,
    across_sem,
    gather_sem,
    share_send_sem,
    share_recv_sem,
    rows_send_sem,
    rows_recv_sem,
    partial_send_sem,
    partial_recv_sem,
):
    block, replica = lax.axis_index("blk"), lax.axis_index("rep")
    groups = blocks // members
    group, member = block // members, lax.rem(block, members)
    tile_side, hidden = grad_out_ref.shape
    slots = listed_ref.shape[1]
    depth = listed_ref.shape[2]
    share = part_ref.shape[0]
    piece = share // members
    halves = hidden // LANES

    def member_device(step):
        return (group * members + lax.rem(member + step, members), replica)

    def across_device(step):
        return (lax.rem(group + step, groups) * members + member, replica)

    def near_device(offset):
        return (lax.rem(block + offset + blocks, blocks), replica)

    def replica_device(step):
        return (block, lax.rem(replica + step, replicas))

    def piece_rows(index):
        return pl.ds(pl.multiple_of(index * piece, piece), piece)

    def share_rows(index):
        return pl.ds(pl.multiple_of(index * share, share), share)

    barrier = pltpu.get_barrier_semaphore()
    greeted = [replica_device(step) for step in range(1, replicas)]
    greeted += [member_device(step) for step in range(1, members)]
    if groups > 1:
        greeted += [across_device(step) for step in range(1, groups)]
        greeted += [near_device(offset) for offset in offsets]
    for target in greeted:
        pl.semaphore_signal(barrier, inc=1, device_id=target, device_id_type=MESH)

    loads = [
        pltpu.make_async_copy(source, target, load_sem.at[index])
        for index, (source, target) in enumerate(
            (
                (grad_out_hbm, grad_out_ref),
                (preact_hbm, preact_ref),
                (aggregated_hbm, aggregated_ref),
                (weight_hbm, weight_ref),
            )
        )
    ]
    sources = [block] + [lax.rem(block - offset + blocks, blocks) for offset in offsets]
    for index, source in enumerate(sources):
        loads.append(
            pltpu.make_async_copy(
                neighbors_hbm.at[0, 0, source], listed_ref.at[index], load_sem.at[4 + index]
            )
        )
    for load in loads:
        load.start()

    inverse = 1.0 / jnp.sqrt(degree_ref[...].astype(jnp.float32))
    inverse = jnp.transpose(jnp.broadcast_to(inverse, (tile_side, tile_side)))[:, :1]

    loads[0].wait()
    loads[1].wait()
    loads[2].wait()
    grad_pre = jnp.where(
        preact_ref[...].astype(jnp.float32) > 0, grad_out_ref[...].astype(jnp.float32), 0.0
    ).astype(jnp.bfloat16)
    local = lax.dot_general(
        aggregated_ref[...], grad_pre, (((0,), (0,)), ((), ())), preferred_element_type=jnp.float32
    )
    for half in range(halves):
        rows = pl.ds(half * hidden, hidden)
        columns = local[:, half * LANES : (half + 1) * LANES]
        local_ref[rows] = columns
    loads[3].wait()
    backward = lax.dot_general(
        grad_pre, weight_ref[...], (((1,), (1,)), ((), ())), preferred_element_type=jnp.float32
    )
    rows_ref[pl.ds(0, tile_side)] = (backward * inverse).astype(jnp.bfloat16)

    pl.semaphore_wait(barrier, len(greeted))

    shared_copies = []
    for step in range(1, replicas):
        copy = pltpu.make_async_remote_copy(
            src_ref=local_ref.at[share_rows(lax.rem(replica + step, replicas))],
            dst_ref=shared_ref.at[pl.ds((step - 1) * share, share)],
            send_sem=shared_send_sem.at[step - 1],
            recv_sem=shared_recv_sem.at[step - 1],
            device_id=replica_device(step),
            device_id_type=MESH,
        )
        copy.start()
        shared_copies.append(copy)

    row_copies = []

    def send_rows(index):
        copy = pltpu.make_async_remote_copy(
            src_ref=rows_ref.at[pl.ds(0, tile_side)],
            dst_ref=rows_ref.at[pl.ds((index + 1) * tile_side, tile_side)],
            send_sem=rows_send_sem.at[index],
            recv_sem=rows_recv_sem.at[index],
            device_id=near_device(offsets[index]),
            device_id_type=MESH,
        )
        copy.start()
        row_copies.append(copy)

    early = len(offsets) // 2
    for index in range(early):
        send_rows(index)

    positions = lax.broadcasted_iota(jnp.int32, (tile_side, tile_side), 0)

    def build_tiles(index):
        source = sources[index]
        loads[4 + index].wait()
        totals = [jnp.zeros((tile_side, tile_side), jnp.float32) for _ in range(replicas)]
        for slot in range(slots):
            counted = jnp.zeros((tile_side, tile_side), jnp.float32)
            for entry in range(depth):
                listed = listed_ref[index, slot, pl.ds(entry, 1), :]
                counted += jnp.where(listed == positions, 1.0, 0.0)
            column = column_ref[0, 0, slot, source]
            present = slot < count_ref[0, 0, source]
            for step in range(replicas):
                here = jnp.logical_and(present, column == lax.rem(replica + step, replicas))
                totals[step] += counted * jnp.where(here, 1.0, 0.0)
        for step in range(replicas):
            tiles_ref[
                pl.ds(step * tile_side, tile_side), pl.ds(index * tile_side, tile_side)
            ] = totals[step].astype(jnp.bfloat16)

    def product(first_row, row_count, first_source, source_count):
        return jnp.dot(
            tiles_ref[
                pl.ds(first_row * tile_side, row_count * tile_side),
                pl.ds(first_source * tile_side, source_count * tile_side),
            ],
            rows_ref[pl.ds(first_source * tile_side, source_count * tile_side)],
            preferred_element_type=jnp.float32,
        )

    def wait_all(ref, sem, count):
        rows = ref.at[pl.ds(0, count * piece)]
        pltpu.make_async_copy(rows, rows, sem).wait()

    for index in range(2):
        build_tiles(index)

    mine = local_ref[share_rows(replica)]
    for step, copy in enumerate(shared_copies):
        copy.wait_recv()
        mine += shared_ref[pl.ds(step * share, share)]
    mine_ref[...] = mine
    part_ref[...] = mine.astype(jnp.bfloat16)
    for step in range(1, members):
        pltpu.make_async_remote_copy(
            src_ref=part_ref.at[piece_rows(lax.rem(member + step, members))],
            dst_ref=spread_ref.at[piece_rows(step - 1)],
            send_sem=spread_sem.at[0],
            recv_sem=spread_sem.at[1],
            device_id=member_device(step),
            device_id_type=MESH,
        ).start()
    for index in range(early, len(offsets)):
        send_rows(index)
    for index in range(2, len(sources)):
        build_tiles(index)

    wait_all(spread_ref, spread_sem.at[1], members - 1)
    reduced = mine_ref[piece_rows(member)]
    for step in range(members - 1):
        reduced += spread_ref[pl.ds(step * piece, piece)].astype(jnp.float32)

    if groups > 1:
        across_ref[0] = reduced
        across_copies = []
        for step in range(1, groups):
            copy = pltpu.make_async_remote_copy(
                src_ref=across_ref.at[0],
                dst_ref=across_ref.at[step],
                send_sem=across_sem.at[0, step],
                recv_sem=across_sem.at[1, step],
                device_id=across_device(step),
                device_id_type=MESH,
            )
            copy.start()
            across_copies.append(copy)
        for step in range(1, groups):
            across_copies[step - 1].wait()
            reduced += across_ref[step]

    base = replica * share + member * piece
    own_piece = pl.ds(pl.multiple_of(base, piece), piece)
    gathered_ref[own_piece] = reduced.astype(jnp.bfloat16)
    for step in range(1, members):
        pltpu.make_async_remote_copy(
            src_ref=gathered_ref.at[own_piece],
            dst_ref=gathered_ref.at[own_piece],
            send_sem=gather_sem.at[0],
            recv_sem=gather_sem.at[1],
            device_id=member_device(step),
            device_id_type=MESH,
        ).start()

    for copy in row_copies:
        copy.wait_recv()
    partial_copies = []
    if replicas > 1:
        partial_ref[...] = product(1, replicas - 1, 0, len(sources))
        for step in range(1, replicas):
            copy = pltpu.make_async_remote_copy(
                src_ref=partial_ref.at[pl.ds((step - 1) * tile_side, tile_side)],
                dst_ref=landed_ref.at[pl.ds((step - 1) * tile_side, tile_side)],
                send_sem=partial_send_sem.at[step - 1],
                recv_sem=partial_recv_sem.at[step - 1],
                device_id=replica_device(step),
                device_id_type=MESH,
            )
            copy.start()
            partial_copies.append(copy)
    wait_all(gathered_ref, gather_sem.at[1], members - 1)
    share_copies = []
    for step in range(1, replicas):
        copy = pltpu.make_async_remote_copy(
            src_ref=gathered_ref.at[share_rows(replica)],
            dst_ref=gathered_ref.at[share_rows(replica)],
            send_sem=share_send_sem.at[step - 1],
            recv_sem=share_recv_sem.at[step - 1],
            device_id=replica_device(step),
            device_id_type=MESH,
        )
        copy.start()
        share_copies.append(copy)
    owned = product(0, 1, 0, len(sources))
    for step, copy in enumerate(partial_copies):
        copy.wait_recv()
        owned += landed_ref[pl.ds(step * tile_side, tile_side)]
    features_ref[...] = (owned * inverse).astype(jnp.bfloat16)

    for copy in share_copies:
        copy.wait_recv()
    raw = gathered_ref[...].astype(jnp.float32)
    total = jnp.sum(jnp.sum(raw * raw, axis=0, keepdims=True), axis=1, keepdims=True)
    scale = jnp.minimum(1.0, 128.0 / jnp.sqrt(total + 1e-06))
    for half in range(halves):
        weight_out_ref[:, pl.ds(half * LANES, LANES)] = (
            raw[half * hidden : (half + 1) * hidden] * scale
        )

    wait_all(spread_ref, spread_sem.at[0], members - 1)
    wait_all(gathered_ref, gather_sem.at[0], members - 1)
    for copy in shared_copies + row_copies + partial_copies + share_copies:
        copy.wait_send()


def on_device(
    blocks, replicas, grad_out, preact, aggregated, weight, degree, neighbors, tile_col, tile_count
):
    tile_side, hidden = grad_out.shape
    slots, depth = neighbors.shape[3], neighbors.shape[4]
    packed = hidden * hidden // LANES
    share = packed // replicas
    members = min(blocks, share // PACKED_ROWS)
    groups = blocks // members
    piece = share // members
    offsets = []
    for distance in range(1, REACH + 1):
        for offset in (distance, -distance):
            if offset % blocks and offset % blocks not in [o % blocks for o in offsets]:
                offsets.append(offset)
    near = len(offsets) + 1
    others = max(replicas - 1, 1)
    hbm = pl.BlockSpec(memory_space=pltpu.HBM)
    vmem = pl.BlockSpec(memory_space=pltpu.VMEM)
    smem = pl.BlockSpec(memory_space=pltpu.SMEM)
    return pl.pallas_call(
        functools.partial(kernel, blocks, replicas, members, tuple(offsets)),
        out_shape=(
            jax.ShapeDtypeStruct((tile_side, hidden), jnp.bfloat16),
            jax.ShapeDtypeStruct((hidden, hidden), jnp.float32),
        ),
        in_specs=[hbm, hbm, hbm, hbm, vmem, hbm, smem, smem],
        out_specs=(vmem, vmem),
        scratch_shapes=[
            pltpu.VMEM((tile_side, hidden), jnp.bfloat16),
            pltpu.VMEM((tile_side, hidden), jnp.bfloat16),
            pltpu.VMEM((tile_side, hidden), jnp.bfloat16),
            pltpu.VMEM((hidden, hidden), jnp.bfloat16),
            pltpu.VMEM((near, slots, depth, tile_side), jnp.int32),
            pltpu.VMEM((packed, LANES), jnp.float32),
            pltpu.VMEM((others * share, LANES), jnp.float32),
            pltpu.VMEM((share, LANES), jnp.float32),
            pltpu.VMEM((share, LANES), jnp.bfloat16),
            pltpu.VMEM((share, LANES), jnp.bfloat16),
            pltpu.VMEM((groups, piece, LANES), jnp.float32),
            pltpu.VMEM((packed, LANES), jnp.bfloat16),
            pltpu.VMEM((near * tile_side, hidden), jnp.bfloat16),
            pltpu.VMEM((replicas * tile_side, near * tile_side), jnp.bfloat16),
            pltpu.VMEM((others * tile_side, hidden), jnp.float32),
            pltpu.VMEM((others * tile_side, hidden), jnp.float32),
            pltpu.SemaphoreType.DMA((4 + near,)),
            pltpu.SemaphoreType.DMA((others,)),
            pltpu.SemaphoreType.DMA((others,)),
            pltpu.SemaphoreType.DMA((2,)),
            pltpu.SemaphoreType.DMA((2, groups)),
            pltpu.SemaphoreType.DMA((2,)),
            pltpu.SemaphoreType.DMA((others,)),
            pltpu.SemaphoreType.DMA((others,)),
            pltpu.SemaphoreType.DMA((near,)),
            pltpu.SemaphoreType.DMA((near,)),
            pltpu.SemaphoreType.DMA((others,)),
            pltpu.SemaphoreType.DMA((others,)),
        ],
        compiler_params=pltpu.CompilerParams(
            collective_id=0, has_side_effects=True, vmem_limit_bytes=63 * 1024 * 1024
        ),
    )(
        grad_out,
        preact,
        aggregated,
        weight,
        degree.reshape(1, tile_side),
        neighbors,
        jnp.swapaxes(tile_col, 2, 3),
        tile_count,
    )


def solution(mesh):
    return jax.shard_map(
        functools.partial(on_device, mesh.shape["blk"], mesh.shape["rep"]),
        mesh=mesh,
        in_specs=(
            P(("blk", "rep"), None),
            P(("blk", "rep"), None),
            P(("blk", "rep"), None),
            P(),
            P(("blk", "rep")),
            P("blk", "rep", None, None, None, None),
            P("blk", "rep", None, None),
            P("blk", "rep", None),
        ),
        out_specs=(P(("blk", "rep"), None), P()),
        check_vma=False,
    )
```

```python
import functools

import jax
import jax.numpy as jnp
from jax import lax
from jax.experimental import pallas as pl
from jax.experimental.pallas import tpu as pltpu
from jax.sharding import PartitionSpec as P

MESH = pl.DeviceIdType.MESH
REACH = 2
LANES = 128
PACKED_ROWS = 16


def kernel(
    blocks,
    replicas,
    members,
    offsets,
    grad_out_hbm,
    preact_hbm,
    aggregated_hbm,
    weight_hbm,
    degree_ref,
    neighbors_hbm,
    column_ref,
    count_ref,
    features_ref,
    weight_out_ref,
    grad_out_ref,
    preact_ref,
    aggregated_ref,
    weight_ref,
    listed_ref,
    local_ref,
    shared_ref,
    mine_ref,
    part_ref,
    spread_ref,
    across_ref,
    gathered_ref,
    rows_ref,
    tiles_ref,
    begun_ref,
    partial_ref,
    landed_ref,
    load_sem,
    shared_send_sem,
    shared_recv_sem,
    spread_sem,
    across_sem,
    gather_sem,
    share_send_sem,
    share_recv_sem,
    rows_send_sem,
    rows_recv_sem,
    partial_send_sem,
    partial_recv_sem,
):
    block, replica = lax.axis_index("blk"), lax.axis_index("rep")
    groups = blocks // members
    group, member = block // members, lax.rem(block, members)
    tile_side, hidden = grad_out_ref.shape
    slots = listed_ref.shape[1]
    depth = listed_ref.shape[2]
    share = part_ref.shape[0]
    piece = share // members
    halves = hidden // LANES

    def member_device(step):
        return (group * members + lax.rem(member + step, members), replica)

    def across_device(step):
        return (lax.rem(group + step, groups) * members + member, replica)

    def near_device(offset):
        return (lax.rem(block + offset + blocks, blocks), replica)

    def replica_device(step):
        return (block, lax.rem(replica + step, replicas))

    def piece_rows(index):
        return pl.ds(pl.multiple_of(index * piece, piece), piece)

    def share_rows(index):
        return pl.ds(pl.multiple_of(index * share, share), share)

    barrier = pltpu.get_barrier_semaphore()
    greeted = [replica_device(step) for step in range(1, replicas)]
    greeted += [member_device(step) for step in range(1, members)]
    if groups > 1:
        greeted += [across_device(step) for step in range(1, groups)]
        greeted += [near_device(offset) for offset in offsets]
    for target in greeted:
        pl.semaphore_signal(barrier, inc=1, device_id=target, device_id_type=MESH)

    loads = [
        pltpu.make_async_copy(source, target, load_sem.at[index])
        for index, (source, target) in enumerate(
            (
                (grad_out_hbm, grad_out_ref),
                (preact_hbm, preact_ref),
                (aggregated_hbm, aggregated_ref),
                (weight_hbm, weight_ref),
            )
        )
    ]
    sources = [block] + [lax.rem(block - offset + blocks, blocks) for offset in offsets]
    for index, source in enumerate(sources):
        loads.append(
            pltpu.make_async_copy(
                neighbors_hbm.at[0, 0, source], listed_ref.at[index], load_sem.at[4 + index]
            )
        )
    for load in loads:
        load.start()

    inverse = 1.0 / jnp.sqrt(degree_ref[...].astype(jnp.float32))
    inverse = jnp.transpose(jnp.broadcast_to(inverse, (tile_side, tile_side)))[:, :1]

    loads[0].wait()
    loads[1].wait()
    grad_pre = jnp.where(
        preact_ref[...].astype(jnp.float32) > 0, grad_out_ref[...].astype(jnp.float32), 0.0
    ).astype(jnp.bfloat16)
    loads[3].wait()
    backward = lax.dot_general(
        grad_pre, weight_ref[...], (((1,), (1,)), ((), ())), preferred_element_type=jnp.float32
    )
    rows_ref[pl.ds(0, tile_side)] = (backward * inverse).astype(jnp.bfloat16)

    pl.semaphore_wait(barrier, len(greeted))

    row_copies = []

    def send_rows(index):
        copy = pltpu.make_async_remote_copy(
            src_ref=rows_ref.at[pl.ds(0, tile_side)],
            dst_ref=rows_ref.at[pl.ds((index + 1) * tile_side, tile_side)],
            send_sem=rows_send_sem.at[index],
            recv_sem=rows_recv_sem.at[index],
            device_id=near_device(offsets[index]),
            device_id_type=MESH,
        )
        copy.start()
        row_copies.append(copy)

    for index in range(len(offsets)):
        send_rows(index)

    loads[2].wait()
    local = lax.dot_general(
        aggregated_ref[...], grad_pre, (((0,), (0,)), ((), ())), preferred_element_type=jnp.float32
    )
    for half in range(halves):
        rows = pl.ds(half * hidden, hidden)
        columns = local[:, half * LANES : (half + 1) * LANES]
        local_ref[rows] = columns
    shared_copies = []
    for step in range(1, replicas):
        copy = pltpu.make_async_remote_copy(
            src_ref=local_ref.at[share_rows(lax.rem(replica + step, replicas))],
            dst_ref=shared_ref.at[pl.ds((step - 1) * share, share)],
            send_sem=shared_send_sem.at[step - 1],
            recv_sem=shared_recv_sem.at[step - 1],
            device_id=replica_device(step),
            device_id_type=MESH,
        )
        copy.start()
        shared_copies.append(copy)

    positions = lax.broadcasted_iota(jnp.int32, (tile_side, tile_side), 0)

    def build_tiles(index):
        source = sources[index]
        loads[4 + index].wait()
        totals = [jnp.zeros((tile_side, tile_side), jnp.float32) for _ in range(replicas)]
        for slot in range(slots):
            counted = jnp.zeros((tile_side, tile_side), jnp.float32)
            for entry in range(depth):
                listed = listed_ref[index, slot, pl.ds(entry, 1), :]
                counted += jnp.where(listed == positions, 1.0, 0.0)
            column = column_ref[0, 0, slot, source]
            present = slot < count_ref[0, 0, source]
            for step in range(replicas):
                here = jnp.logical_and(present, column == lax.rem(replica + step, replicas))
                totals[step] += counted * jnp.where(here, 1.0, 0.0)
        for step in range(replicas):
            tiles_ref[
                pl.ds(step * tile_side, tile_side), pl.ds(index * tile_side, tile_side)
            ] = totals[step].astype(jnp.bfloat16)

    def product(first_row, row_count, first_source, source_count):
        return jnp.dot(
            tiles_ref[
                pl.ds(first_row * tile_side, row_count * tile_side),
                pl.ds(first_source * tile_side, source_count * tile_side),
            ],
            rows_ref[pl.ds(first_source * tile_side, source_count * tile_side)],
            preferred_element_type=jnp.float32,
        )

    def wait_all(ref, sem, count):
        rows = ref.at[pl.ds(0, count * piece)]
        pltpu.make_async_copy(rows, rows, sem).wait()

    for index in range(2):
        build_tiles(index)

    mine = local_ref[share_rows(replica)]
    for step, copy in enumerate(shared_copies):
        copy.wait_recv()
        mine += shared_ref[pl.ds(step * share, share)]
    mine_ref[...] = mine
    part_ref[...] = mine.astype(jnp.bfloat16)
    for step in range(1, members):
        pltpu.make_async_remote_copy(
            src_ref=part_ref.at[piece_rows(lax.rem(member + step, members))],
            dst_ref=spread_ref.at[piece_rows(step - 1)],
            send_sem=spread_sem.at[0],
            recv_sem=spread_sem.at[1],
            device_id=member_device(step),
            device_id_type=MESH,
        ).start()
    for index in range(2, len(sources)):
        build_tiles(index)

    wait_all(spread_ref, spread_sem.at[1], members - 1)
    reduced = mine_ref[piece_rows(member)]
    for step in range(members - 1):
        reduced += spread_ref[pl.ds(step * piece, piece)].astype(jnp.float32)

    if groups > 1:
        across_ref[0] = reduced
        across_copies = []
        for step in range(1, groups):
            copy = pltpu.make_async_remote_copy(
                src_ref=across_ref.at[0],
                dst_ref=across_ref.at[step],
                send_sem=across_sem.at[0, step],
                recv_sem=across_sem.at[1, step],
                device_id=across_device(step),
                device_id_type=MESH,
            )
            copy.start()
            across_copies.append(copy)
        for step in range(1, groups):
            across_copies[step - 1].wait()
            reduced += across_ref[step]

    base = replica * share + member * piece
    own_piece = pl.ds(pl.multiple_of(base, piece), piece)
    gathered_ref[own_piece] = reduced.astype(jnp.bfloat16)
    for step in range(1, members):
        pltpu.make_async_remote_copy(
            src_ref=gathered_ref.at[own_piece],
            dst_ref=gathered_ref.at[own_piece],
            send_sem=gather_sem.at[0],
            recv_sem=gather_sem.at[1],
            device_id=member_device(step),
            device_id_type=MESH,
        ).start()

    early = len(sources) // 2 + 1
    for copy in row_copies[: early - 1]:
        copy.wait_recv()
    begun_ref[...] = product(0, replicas, 0, early)
    for copy in row_copies[early - 1 :]:
        copy.wait_recv()
    partial_copies = []
    if replicas > 1:
        others = pl.ds(tile_side, (replicas - 1) * tile_side)
        partial_ref[...] = begun_ref[others] + product(
            1, replicas - 1, early, len(sources) - early
        )
        for step in range(1, replicas):
            copy = pltpu.make_async_remote_copy(
                src_ref=partial_ref.at[pl.ds((step - 1) * tile_side, tile_side)],
                dst_ref=landed_ref.at[pl.ds((step - 1) * tile_side, tile_side)],
                send_sem=partial_send_sem.at[step - 1],
                recv_sem=partial_recv_sem.at[step - 1],
                device_id=replica_device(step),
                device_id_type=MESH,
            )
            copy.start()
            partial_copies.append(copy)
    wait_all(gathered_ref, gather_sem.at[1], members - 1)
    share_copies = []
    for step in range(1, replicas):
        copy = pltpu.make_async_remote_copy(
            src_ref=gathered_ref.at[share_rows(replica)],
            dst_ref=gathered_ref.at[share_rows(replica)],
            send_sem=share_send_sem.at[step - 1],
            recv_sem=share_recv_sem.at[step - 1],
            device_id=replica_device(step),
            device_id_type=MESH,
        )
        copy.start()
        share_copies.append(copy)
    owned = begun_ref[pl.ds(0, tile_side)] + product(0, 1, early, len(sources) - early)
    for step, copy in enumerate(partial_copies):
        copy.wait_recv()
        owned += landed_ref[pl.ds(step * tile_side, tile_side)]
    features_ref[...] = (owned * inverse).astype(jnp.bfloat16)

    for copy in share_copies:
        copy.wait_recv()
    raw = gathered_ref[...].astype(jnp.float32)
    total = jnp.sum(jnp.sum(raw * raw, axis=0, keepdims=True), axis=1, keepdims=True)
    scale = jnp.minimum(1.0, 128.0 / jnp.sqrt(total + 1e-06))
    for half in range(halves):
        weight_out_ref[:, pl.ds(half * LANES, LANES)] = (
            raw[half * hidden : (half + 1) * hidden] * scale
        )

    wait_all(spread_ref, spread_sem.at[0], members - 1)
    wait_all(gathered_ref, gather_sem.at[0], members - 1)
    for copy in shared_copies + row_copies + partial_copies + share_copies:
        copy.wait_send()


def on_device(
    blocks, replicas, grad_out, preact, aggregated, weight, degree, neighbors, tile_col, tile_count
):
    tile_side, hidden = grad_out.shape
    slots, depth = neighbors.shape[3], neighbors.shape[4]
    packed = hidden * hidden // LANES
    share = packed // replicas
    members = min(blocks, share // PACKED_ROWS)
    groups = blocks // members
    piece = share // members
    offsets = []
    for distance in range(REACH, 0, -1):
        for offset in (distance, -distance):
            if offset % blocks and offset % blocks not in [o % blocks for o in offsets]:
                offsets.append(offset)
    near = len(offsets) + 1
    others = max(replicas - 1, 1)
    held = functools.partial(pltpu.with_memory_space_constraint, memory_space=pltpu.HBM)
    hbm = pl.BlockSpec(memory_space=pltpu.HBM)
    vmem = pl.BlockSpec(memory_space=pltpu.VMEM)
    smem = pl.BlockSpec(memory_space=pltpu.SMEM)
    return pl.pallas_call(
        functools.partial(kernel, blocks, replicas, members, tuple(offsets)),
        out_shape=(
            pltpu.VMEM((tile_side, hidden), jnp.bfloat16),
            pltpu.VMEM((hidden, hidden), jnp.float32),
        ),
        in_specs=[hbm, hbm, hbm, hbm, vmem, hbm, smem, smem],
        out_specs=(vmem, vmem),
        scratch_shapes=[
            pltpu.VMEM((tile_side, hidden), jnp.bfloat16),
            pltpu.VMEM((tile_side, hidden), jnp.bfloat16),
            pltpu.VMEM((tile_side, hidden), jnp.bfloat16),
            pltpu.VMEM((hidden, hidden), jnp.bfloat16),
            pltpu.VMEM((near, slots, depth, tile_side), jnp.int32),
            pltpu.VMEM((packed, LANES), jnp.float32),
            pltpu.VMEM((others * share, LANES), jnp.float32),
            pltpu.VMEM((share, LANES), jnp.float32),
            pltpu.VMEM((share, LANES), jnp.bfloat16),
            pltpu.VMEM((share, LANES), jnp.bfloat16),
            pltpu.VMEM((groups, piece, LANES), jnp.float32),
            pltpu.VMEM((packed, LANES), jnp.bfloat16),
            pltpu.VMEM((near * tile_side, hidden), jnp.bfloat16),
            pltpu.VMEM((replicas * tile_side, near * tile_side), jnp.bfloat16),
            pltpu.VMEM((replicas * tile_side, hidden), jnp.float32),
            pltpu.VMEM((others * tile_side, hidden), jnp.float32),
            pltpu.VMEM((others * tile_side, hidden), jnp.float32),
            pltpu.SemaphoreType.DMA((4 + near,)),
            pltpu.SemaphoreType.DMA((others,)),
            pltpu.SemaphoreType.DMA((others,)),
            pltpu.SemaphoreType.DMA((2,)),
            pltpu.SemaphoreType.DMA((2, groups)),
            pltpu.SemaphoreType.DMA((2,)),
            pltpu.SemaphoreType.DMA((others,)),
            pltpu.SemaphoreType.DMA((others,)),
            pltpu.SemaphoreType.DMA((near,)),
            pltpu.SemaphoreType.DMA((near,)),
            pltpu.SemaphoreType.DMA((others,)),
            pltpu.SemaphoreType.DMA((others,)),
        ],
        compiler_params=pltpu.CompilerParams(
            collective_id=0, has_side_effects=True, vmem_limit_bytes=32 * 1024 * 1024
        ),
    )(
        held(grad_out),
        held(preact),
        held(aggregated),
        held(weight),
        held(degree.reshape(1, tile_side)),
        held(neighbors),
        held(jnp.swapaxes(tile_col, 2, 3)),
        held(tile_count),
    )


def solution(mesh):
    return jax.shard_map(
        functools.partial(on_device, mesh.shape["blk"], mesh.shape["rep"]),
        mesh=mesh,
        in_specs=(
            P(("blk", "rep"), None),
            P(("blk", "rep"), None),
            P(("blk", "rep"), None),
            P(),
            P(("blk", "rep")),
            P("blk", "rep", None, None, None, None),
            P("blk", "rep", None, None),
            P("blk", "rep", None),
        ),
        out_specs=(P(("blk", "rep"), None), P()),
        check_vma=False,
    )
```

```python
import functools

import jax
import jax.numpy as jnp
from jax import lax
from jax.experimental import pallas as pl
from jax.experimental.pallas import tpu as pltpu
from jax.sharding import PartitionSpec as P

MESH = pl.DeviceIdType.MESH
REACH = 2
LANES = 128
PACKED_ROWS = 16


def kernel(
    blocks,
    replicas,
    members,
    offsets,
    grad_out_hbm,
    preact_hbm,
    aggregated_hbm,
    weight_hbm,
    degree_ref,
    neighbors_hbm,
    column_ref,
    count_ref,
    features_ref,
    weight_out_ref,
    grad_out_ref,
    preact_ref,
    aggregated_ref,
    weight_ref,
    listed_ref,
    local_ref,
    part_ref,
    spread_ref,
    across_ref,
    gathered_ref,
    rows_ref,
    tiles_ref,
    begun_ref,
    partial_ref,
    landed_ref,
    load_sem,
    spread_sem,
    across_sem,
    gather_sem,
    rows_send_sem,
    rows_recv_sem,
    partial_send_sem,
    partial_recv_sem,
):
    block, replica = lax.axis_index("blk"), lax.axis_index("rep")
    me = block * replicas + replica
    groups = blocks * replicas // members
    group, member = me // members, lax.rem(me, members)
    tile_side, hidden = grad_out_ref.shape
    slots = listed_ref.shape[1]
    depth = listed_ref.shape[2]
    piece = part_ref.shape[0] // members
    halves = hidden // LANES

    def device(flat):
        return (flat // replicas, lax.rem(flat, replicas))

    def group_peer(step):
        return group * members + lax.rem(member + step, members)

    def across_peer(step):
        return lax.rem(group + step, groups) * members + member

    def near_device(offset):
        return (lax.rem(block + offset + blocks, blocks), replica)

    def replica_device(step):
        return (block, lax.rem(replica + step, replicas))

    def piece_rows(index):
        return pl.ds(pl.multiple_of(index * piece, piece), piece)

    loads = [
        pltpu.make_async_copy(source, target, load_sem.at[index])
        for index, (source, target) in enumerate(
            (
                (grad_out_hbm, grad_out_ref),
                (preact_hbm, preact_ref),
                (aggregated_hbm, aggregated_ref),
                (weight_hbm, weight_ref),
            )
        )
    ]
    sources = [block] + [lax.rem(block - offset + blocks, blocks) for offset in offsets]
    for index, source in enumerate(sources):
        loads.append(
            pltpu.make_async_copy(
                neighbors_hbm.at[0, 0, source], listed_ref.at[index], load_sem.at[4 + index]
            )
        )
    for load in loads:
        load.start()

    barrier = pltpu.get_barrier_semaphore()

    def greet(target):
        pl.semaphore_signal(barrier, inc=1, device_id=target, device_id_type=MESH)

    def greet_member(step, carry):
        greet(device(group_peer(step)))
        return carry

    lax.fori_loop(1, members, greet_member, 0)
    greeted = members - 1
    if groups > 1:
        for step in range(1, groups):
            greet(device(across_peer(step)))
        for offset in offsets:
            greet(near_device(offset))
        for step in range(1, replicas):
            greet(replica_device(step))
        greeted += groups - 1 + len(offsets) + replicas - 1

    inverse = 1.0 / jnp.sqrt(degree_ref[...].astype(jnp.float32))
    inverse = jnp.transpose(jnp.broadcast_to(inverse, (tile_side, tile_side)))[:, :1]

    loads[0].wait()
    loads[1].wait()
    loads[2].wait()
    grad_pre = jnp.where(
        preact_ref[...].astype(jnp.float32) > 0, grad_out_ref[...].astype(jnp.float32), 0.0
    ).astype(jnp.bfloat16)
    local = lax.dot_general(
        aggregated_ref[...], grad_pre, (((0,), (0,)), ((), ())), preferred_element_type=jnp.float32
    )
    for half in range(halves):
        rows = pl.ds(half * hidden, hidden)
        columns = local[:, half * LANES : (half + 1) * LANES]
        local_ref[rows] = columns
        part_ref[rows] = columns.astype(jnp.bfloat16)
    loads[3].wait()
    backward = lax.dot_general(
        grad_pre, weight_ref[...], (((1,), (1,)), ((), ())), preferred_element_type=jnp.float32
    )
    rows_ref[pl.ds(0, tile_side)] = (backward * inverse).astype(jnp.bfloat16)

    pl.semaphore_wait(barrier, greeted)

    def send_piece(step, carry):
        peer = group_peer(step)
        pltpu.make_async_remote_copy(
            src_ref=part_ref.at[piece_rows(lax.rem(peer, members))],
            dst_ref=spread_ref.at[piece_rows(step - 1)],
            send_sem=spread_sem.at[0],
            recv_sem=spread_sem.at[1],
            device_id=device(peer),
            device_id_type=MESH,
        ).start()
        return carry

    lax.fori_loop(1, members, send_piece, 0)

    row_copies = []
    for index, offset in enumerate(offsets):
        copy = pltpu.make_async_remote_copy(
            src_ref=rows_ref.at[pl.ds(0, tile_side)],
            dst_ref=rows_ref.at[pl.ds((index + 1) * tile_side, tile_side)],
            send_sem=rows_send_sem.at[index],
            recv_sem=rows_recv_sem.at[index],
            device_id=near_device(offset),
            device_id_type=MESH,
        )
        copy.start()
        row_copies.append(copy)

    chunk = tile_side // 2
    positions = lax.broadcasted_iota(jnp.int32, (chunk, tile_side), 0)
    for load in loads[4:]:
        load.wait()

    def build_tiles(index, carry):
        source = sources[0]
        for other in range(1, len(sources)):
            source = jnp.where(index == other, sources[other], source)
        lanes = pl.ds(pl.multiple_of(index * tile_side, tile_side), tile_side)
        weights = []
        for slot in range(slots):
            column = column_ref[0, 0, slot, source]
            present = slot < count_ref[0, 0, source]
            weights.append([
                jnp.where(
                    jnp.logical_and(present, column == lax.rem(replica + step, replicas)), 1.0, 0.0
                )
                for step in range(replicas)
            ])
        for start in range(0, tile_side, chunk):
            totals = [None] * replicas
            for slot in range(slots):
                counted = jnp.zeros((chunk, tile_side), jnp.float32)
                for entry in range(depth):
                    listed = listed_ref[index, slot, pl.ds(entry, 1), :] - start
                    counted += jnp.where(listed == positions, 1.0, 0.0)
                for step in range(replicas):
                    term = counted * weights[slot][step]
                    totals[step] = term if slot == 0 else totals[step] + term
            for step in range(replicas):
                tiles_ref[pl.ds(step * tile_side + start, chunk), lanes] = totals[step].astype(
                    jnp.bfloat16
                )
        return carry

    lax.fori_loop(0, len(sources), build_tiles, 0)

    def product(first_row, row_count, first_source, source_count):
        return jnp.dot(
            tiles_ref[
                pl.ds(first_row * tile_side, row_count * tile_side),
                pl.ds(first_source * tile_side, source_count * tile_side),
            ],
            rows_ref[pl.ds(first_source * tile_side, source_count * tile_side)],
            preferred_element_type=jnp.float32,
        )

    def wait_all(ref, sem, count):
        rows = ref.at[pl.ds(0, count * piece)]
        pltpu.make_async_copy(rows, rows, sem).wait()

    wait_all(spread_ref, spread_sem.at[1], members - 1)
    reduced = local_ref[piece_rows(member)]
    for step in range(members - 1):
        reduced += spread_ref[pl.ds(step * piece, piece)].astype(jnp.float32)

    if groups > 1:
        across_ref[0] = reduced
        across_copies = []
        for step in range(1, groups):
            copy = pltpu.make_async_remote_copy(
                src_ref=across_ref.at[0],
                dst_ref=across_ref.at[step],
                send_sem=across_sem.at[0, step],
                recv_sem=across_sem.at[1, step],
                device_id=device(across_peer(step)),
                device_id_type=MESH,
            )
            copy.start()
            across_copies.append(copy)
        for step in range(1, groups):
            across_copies[step - 1].wait()
            reduced += across_ref[step]

    gathered_ref[piece_rows(member)] = reduced.astype(jnp.bfloat16)

    def send_reduced(step, carry):
        pltpu.make_async_remote_copy(
            src_ref=gathered_ref.at[piece_rows(member)],
            dst_ref=gathered_ref.at[piece_rows(member)],
            send_sem=gather_sem.at[0],
            recv_sem=gather_sem.at[1],
            device_id=device(group_peer(step)),
            device_id_type=MESH,
        ).start()
        return carry

    lax.fori_loop(1, members, send_reduced, 0)

    early = len(sources) // 2 + 1
    for copy in row_copies[: early - 1]:
        copy.wait_recv()
    begun_ref[...] = product(0, replicas, 0, early)
    for copy in row_copies[early - 1 :]:
        copy.wait_recv()
    partial_copies = []
    if replicas > 1:
        others = pl.ds(tile_side, (replicas - 1) * tile_side)
        partial_ref[...] = begun_ref[others] + product(
            1, replicas - 1, early, len(sources) - early
        )
        for step in range(1, replicas):
            copy = pltpu.make_async_remote_copy(
                src_ref=partial_ref.at[pl.ds((step - 1) * tile_side, tile_side)],
                dst_ref=landed_ref.at[pl.ds((step - 1) * tile_side, tile_side)],
                send_sem=partial_send_sem.at[step - 1],
                recv_sem=partial_recv_sem.at[step - 1],
                device_id=replica_device(step),
                device_id_type=MESH,
            )
            copy.start()
            partial_copies.append(copy)
    owned = begun_ref[pl.ds(0, tile_side)] + product(0, 1, early, len(sources) - early)
    for step, copy in enumerate(partial_copies):
        copy.wait_recv()
        owned += landed_ref[pl.ds(step * tile_side, tile_side)]
    features_ref[...] = (owned * inverse).astype(jnp.bfloat16)

    wait_all(gathered_ref, gather_sem.at[1], members - 1)
    raw = gathered_ref[...].astype(jnp.float32)
    total = jnp.sum(jnp.sum(raw * raw, axis=0, keepdims=True), axis=1, keepdims=True)
    scale = jnp.minimum(1.0, 128.0 / jnp.sqrt(total + 1e-06))
    for half in range(halves):
        weight_out_ref[:, pl.ds(half * LANES, LANES)] = (
            raw[half * hidden : (half + 1) * hidden] * scale
        )

    wait_all(spread_ref, spread_sem.at[0], members - 1)
    wait_all(gathered_ref, gather_sem.at[0], members - 1)
    for copy in row_copies + partial_copies:
        copy.wait_send()


def on_device(
    blocks, replicas, grad_out, preact, aggregated, weight, degree, neighbors, tile_col, tile_count
):
    tile_side, hidden = grad_out.shape
    slots, depth = neighbors.shape[3], neighbors.shape[4]
    packed = hidden * hidden // LANES
    members = min(blocks * replicas, packed // PACKED_ROWS)
    groups = blocks * replicas // members
    piece = packed // members
    offsets = []
    for distance in range(REACH, 0, -1):
        for offset in (distance, -distance):
            if offset % blocks and offset % blocks not in [o % blocks for o in offsets]:
                offsets.append(offset)
    near = len(offsets) + 1
    others = max(replicas - 1, 1)
    held = functools.partial(pltpu.with_memory_space_constraint, memory_space=pltpu.HBM)
    hbm = pl.BlockSpec(memory_space=pltpu.HBM)
    vmem = pl.BlockSpec(memory_space=pltpu.VMEM)
    smem = pl.BlockSpec(memory_space=pltpu.SMEM)
    return pl.pallas_call(
        functools.partial(kernel, blocks, replicas, members, tuple(offsets)),
        out_shape=(
            pltpu.VMEM((tile_side, hidden), jnp.bfloat16),
            pltpu.VMEM((hidden, hidden), jnp.float32),
        ),
        in_specs=[hbm, hbm, hbm, hbm, vmem, hbm, smem, smem],
        out_specs=(vmem, vmem),
        scratch_shapes=[
            pltpu.VMEM((tile_side, hidden), jnp.bfloat16),
            pltpu.VMEM((tile_side, hidden), jnp.bfloat16),
            pltpu.VMEM((tile_side, hidden), jnp.bfloat16),
            pltpu.VMEM((hidden, hidden), jnp.bfloat16),
            pltpu.VMEM((near, slots, depth, tile_side), jnp.int32),
            pltpu.VMEM((packed, LANES), jnp.float32),
            pltpu.VMEM((packed, LANES), jnp.bfloat16),
            pltpu.VMEM((packed, LANES), jnp.bfloat16),
            pltpu.VMEM((groups, piece, LANES), jnp.float32),
            pltpu.VMEM((packed, LANES), jnp.bfloat16),
            pltpu.VMEM((near * tile_side, hidden), jnp.bfloat16),
            pltpu.VMEM((replicas * tile_side, near * tile_side), jnp.bfloat16),
            pltpu.VMEM((replicas * tile_side, hidden), jnp.float32),
            pltpu.VMEM((others * tile_side, hidden), jnp.float32),
            pltpu.VMEM((others * tile_side, hidden), jnp.float32),
            pltpu.SemaphoreType.DMA((4 + near,)),
            pltpu.SemaphoreType.DMA((2,)),
            pltpu.SemaphoreType.DMA((2, groups)),
            pltpu.SemaphoreType.DMA((2,)),
            pltpu.SemaphoreType.DMA((near,)),
            pltpu.SemaphoreType.DMA((near,)),
            pltpu.SemaphoreType.DMA((others,)),
            pltpu.SemaphoreType.DMA((others,)),
        ],
        compiler_params=pltpu.CompilerParams(
            collective_id=0, has_side_effects=True, vmem_limit_bytes=32 * 1024 * 1024
        ),
    )(
        held(grad_out),
        held(preact),
        held(aggregated),
        held(weight),
        held(degree.reshape(1, tile_side)),
        held(neighbors),
        held(jnp.swapaxes(tile_col, 2, 3)),
        held(tile_count),
    )


def solution(mesh):
    return jax.shard_map(
        functools.partial(on_device, mesh.shape["blk"], mesh.shape["rep"]),
        mesh=mesh,
        in_specs=(
            P(("blk", "rep"), None),
            P(("blk", "rep"), None),
            P(("blk", "rep"), None),
            P(),
            P(("blk", "rep")),
            P("blk", "rep", None, None, None, None),
            P("blk", "rep", None, None),
            P("blk", "rep", None),
        ),
        out_specs=(P(("blk", "rep"), None), P()),
        check_vma=False,
    )
```

```python
import functools

import jax
import jax.numpy as jnp
from jax import lax
from jax.experimental import pallas as pl
from jax.experimental.pallas import tpu as pltpu
from jax.sharding import PartitionSpec as P

MESH = pl.DeviceIdType.MESH
REACH = 2
LANES = 128
PACKED_ROWS = 16


def kernel(
    blocks,
    replicas,
    members,
    offsets,
    grad_out_hbm,
    preact_hbm,
    aggregated_hbm,
    weight_hbm,
    degree_ref,
    neighbors_hbm,
    column_ref,
    count_ref,
    features_ref,
    weight_out_ref,
    grad_out_ref,
    preact_ref,
    aggregated_ref,
    weight_ref,
    listed_ref,
    local_ref,
    part_ref,
    spread_ref,
    across_ref,
    gathered_ref,
    rows_ref,
    tiles_ref,
    begun_ref,
    partial_ref,
    landed_ref,
    load_sem,
    spread_sem,
    across_sem,
    gather_sem,
    rows_send_sem,
    rows_recv_sem,
    partial_send_sem,
    partial_recv_sem,
):
    block, replica = lax.axis_index("blk"), lax.axis_index("rep")
    side = members // replicas
    groups = blocks // side
    group, place = block // side, lax.rem(block, side)
    member = place * replicas + replica
    tile_side, hidden = grad_out_ref.shape
    slots = listed_ref.shape[1]
    depth = listed_ref.shape[2]
    piece = part_ref.shape[0] // members
    halves = hidden // LANES

    def across_device(step):
        return (lax.rem(group + step, groups) * side + place, replica)

    def each_member(act):
        def at_distance(step, carry):
            peer_place = lax.rem(place + step, side)
            for other in range(replicas):
                act(
                    (group * side + peer_place, other),
                    peer_place * replicas + other,
                    (step - 1) * replicas + replica,
                )
            return carry

        lax.fori_loop(1, side, at_distance, 0)
        for step in range(1, replicas):
            other = lax.rem(replica + step, replicas)
            act((block, other), place * replicas + other, (side - 1) * replicas + step - 1)

    def near_device(offset):
        return (lax.rem(block + offset + blocks, blocks), replica)

    def replica_device(step):
        return (block, lax.rem(replica + step, replicas))

    def piece_rows(index):
        return pl.ds(pl.multiple_of(index * piece, piece), piece)

    loads = [
        pltpu.make_async_copy(source, target, load_sem.at[index])
        for index, (source, target) in enumerate(
            (
                (grad_out_hbm, grad_out_ref),
                (preact_hbm, preact_ref),
                (aggregated_hbm, aggregated_ref),
                (weight_hbm, weight_ref),
            )
        )
    ]
    sources = [block] + [lax.rem(block - offset + blocks, blocks) for offset in offsets]
    for index, source in enumerate(sources):
        loads.append(
            pltpu.make_async_copy(
                neighbors_hbm.at[0, 0, source], listed_ref.at[index], load_sem.at[4 + index]
            )
        )
    for load in loads:
        load.start()

    barrier = pltpu.get_barrier_semaphore()

    def greet(target):
        pl.semaphore_signal(barrier, inc=1, device_id=target, device_id_type=MESH)

    each_member(lambda target, index, slot: greet(target))
    greeted = members - 1
    if groups > 1:
        for step in range(1, groups):
            greet(across_device(step))
        for offset in offsets:
            greet(near_device(offset))
        for step in range(1, replicas):
            greet(replica_device(step))
        greeted += groups - 1 + len(offsets) + replicas - 1

    inverse = 1.0 / jnp.sqrt(degree_ref[...].astype(jnp.float32))
    inverse = jnp.transpose(jnp.broadcast_to(inverse, (tile_side, tile_side)))[:, :1]

    loads[0].wait()
    loads[1].wait()
    loads[2].wait()
    grad_pre = jnp.where(
        preact_ref[...].astype(jnp.float32) > 0, grad_out_ref[...].astype(jnp.float32), 0.0
    ).astype(jnp.bfloat16)
    local = lax.dot_general(
        aggregated_ref[...], grad_pre, (((0,), (0,)), ((), ())), preferred_element_type=jnp.float32
    )
    for half in range(halves):
        rows = pl.ds(half * hidden, hidden)
        columns = local[:, half * LANES : (half + 1) * LANES]
        local_ref[rows] = columns
        part_ref[rows] = columns.astype(jnp.bfloat16)
    pl.semaphore_wait(barrier, greeted)

    def send_piece(target, index, slot):
        pltpu.make_async_remote_copy(
            src_ref=part_ref.at[piece_rows(index)],
            dst_ref=spread_ref.at[piece_rows(slot)],
            send_sem=spread_sem.at[0],
            recv_sem=spread_sem.at[1],
            device_id=target,
            device_id_type=MESH,
        ).start()

    each_member(send_piece)

    loads[3].wait()
    backward = lax.dot_general(
        grad_pre, weight_ref[...], (((1,), (1,)), ((), ())), preferred_element_type=jnp.float32
    )
    rows_ref[pl.ds(0, tile_side)] = (backward * inverse).astype(jnp.bfloat16)

    row_copies = []
    for index, offset in enumerate(offsets):
        copy = pltpu.make_async_remote_copy(
            src_ref=rows_ref.at[pl.ds(0, tile_side)],
            dst_ref=rows_ref.at[pl.ds((index + 1) * tile_side, tile_side)],
            send_sem=rows_send_sem.at[index],
            recv_sem=rows_recv_sem.at[index],
            device_id=near_device(offset),
            device_id_type=MESH,
        )
        copy.start()
        row_copies.append(copy)

    chunk = tile_side // 2
    positions = lax.broadcasted_iota(jnp.int32, (chunk, tile_side), 0)
    for load in loads[4:]:
        load.wait()

    def build_tiles(index, carry):
        source = sources[0]
        for other in range(1, len(sources)):
            source = jnp.where(index == other, sources[other], source)
        lanes = pl.ds(pl.multiple_of(index * tile_side, tile_side), tile_side)
        weights = []
        for slot in range(slots):
            column = column_ref[0, 0, slot, source]
            present = slot < count_ref[0, 0, source]
            weights.append([
                jnp.where(
                    jnp.logical_and(present, column == lax.rem(replica + step, replicas)), 1.0, 0.0
                )
                for step in range(replicas)
            ])
        for start in range(0, tile_side, chunk):
            totals = [None] * replicas
            for slot in range(slots):
                counted = jnp.zeros((chunk, tile_side), jnp.float32)
                for entry in range(depth):
                    listed = listed_ref[index, slot, pl.ds(entry, 1), :] - start
                    counted += jnp.where(listed == positions, 1.0, 0.0)
                for step in range(replicas):
                    term = counted * weights[slot][step]
                    totals[step] = term if slot == 0 else totals[step] + term
            for step in range(replicas):
                tiles_ref[pl.ds(step * tile_side + start, chunk), lanes] = totals[step].astype(
                    jnp.bfloat16
                )
        return carry

    lax.fori_loop(0, 2, build_tiles, 0)

    def product(first_row, row_count, first_source, source_count):
        return jnp.dot(
            tiles_ref[
                pl.ds(first_row * tile_side, row_count * tile_side),
                pl.ds(first_source * tile_side, source_count * tile_side),
            ],
            rows_ref[pl.ds(first_source * tile_side, source_count * tile_side)],
            preferred_element_type=jnp.float32,
        )

    def wait_all(ref, sem, count):
        rows = ref.at[pl.ds(0, count * piece)]
        pltpu.make_async_copy(rows, rows, sem).wait()

    wait_all(spread_ref, spread_sem.at[1], members - 1)
    reduced = local_ref[piece_rows(member)]
    for step in range(members - 1):
        reduced += spread_ref[pl.ds(step * piece, piece)].astype(jnp.float32)

    if groups > 1:
        across_ref[0] = reduced
        across_copies = []
        for step in range(1, groups):
            copy = pltpu.make_async_remote_copy(
                src_ref=across_ref.at[0],
                dst_ref=across_ref.at[step],
                send_sem=across_sem.at[0, step],
                recv_sem=across_sem.at[1, step],
                device_id=across_device(step),
                device_id_type=MESH,
            )
            copy.start()
            across_copies.append(copy)
        for step in range(1, groups):
            across_copies[step - 1].wait()
            reduced += across_ref[step]

    gathered_ref[piece_rows(member)] = reduced.astype(jnp.bfloat16)

    def send_reduced(target, index, slot):
        pltpu.make_async_remote_copy(
            src_ref=gathered_ref.at[piece_rows(member)],
            dst_ref=gathered_ref.at[piece_rows(member)],
            send_sem=gather_sem.at[0],
            recv_sem=gather_sem.at[1],
            device_id=target,
            device_id_type=MESH,
        ).start()

    each_member(send_reduced)
    lax.fori_loop(2, len(sources), build_tiles, 0)

    early = len(sources) // 2 + 1
    for copy in row_copies[: early - 1]:
        copy.wait_recv()
    begun_ref[...] = product(0, replicas, 0, early)
    for copy in row_copies[early - 1 :]:
        copy.wait_recv()
    partial_copies = []
    if replicas > 1:
        others = pl.ds(tile_side, (replicas - 1) * tile_side)
        partial_ref[...] = begun_ref[others] + product(
            1, replicas - 1, early, len(sources) - early
        )
        for step in range(1, replicas):
            copy = pltpu.make_async_remote_copy(
                src_ref=partial_ref.at[pl.ds((step - 1) * tile_side, tile_side)],
                dst_ref=landed_ref.at[pl.ds((step - 1) * tile_side, tile_side)],
                send_sem=partial_send_sem.at[step - 1],
                recv_sem=partial_recv_sem.at[step - 1],
                device_id=replica_device(step),
                device_id_type=MESH,
            )
            copy.start()
            partial_copies.append(copy)
    owned = begun_ref[pl.ds(0, tile_side)] + product(0, 1, early, len(sources) - early)
    for step, copy in enumerate(partial_copies):
        copy.wait_recv()
        owned += landed_ref[pl.ds(step * tile_side, tile_side)]
    features_ref[...] = (owned * inverse).astype(jnp.bfloat16)

    wait_all(gathered_ref, gather_sem.at[1], members - 1)
    raw = gathered_ref[...].astype(jnp.float32)
    total = jnp.sum(jnp.sum(raw * raw, axis=0, keepdims=True), axis=1, keepdims=True)
    scale = jnp.minimum(1.0, 128.0 / jnp.sqrt(total + 1e-06))
    for half in range(halves):
        weight_out_ref[:, pl.ds(half * LANES, LANES)] = (
            raw[half * hidden : (half + 1) * hidden] * scale
        )

    wait_all(spread_ref, spread_sem.at[0], members - 1)
    wait_all(gathered_ref, gather_sem.at[0], members - 1)
    for copy in row_copies + partial_copies:
        copy.wait_send()


def on_device(
    blocks, replicas, grad_out, preact, aggregated, weight, degree, neighbors, tile_col, tile_count
):
    tile_side, hidden = grad_out.shape
    slots, depth = neighbors.shape[3], neighbors.shape[4]
    packed = hidden * hidden // LANES
    members = min(blocks * replicas, packed // PACKED_ROWS)
    groups = blocks * replicas // members
    piece = packed // members
    offsets = []
    for distance in range(REACH, 0, -1):
        for offset in (distance, -distance):
            if offset % blocks and offset % blocks not in [o % blocks for o in offsets]:
                offsets.append(offset)
    near = len(offsets) + 1
    others = max(replicas - 1, 1)
    held = functools.partial(pltpu.with_memory_space_constraint, memory_space=pltpu.HBM)
    hbm = pl.BlockSpec(memory_space=pltpu.HBM)
    vmem = pl.BlockSpec(memory_space=pltpu.VMEM)
    smem = pl.BlockSpec(memory_space=pltpu.SMEM)
    return pl.pallas_call(
        functools.partial(kernel, blocks, replicas, members, tuple(offsets)),
        out_shape=(
            pltpu.VMEM((tile_side, hidden), jnp.bfloat16),
            pltpu.VMEM((hidden, hidden), jnp.float32),
        ),
        in_specs=[hbm, hbm, hbm, hbm, vmem, hbm, smem, smem],
        out_specs=(vmem, vmem),
        scratch_shapes=[
            pltpu.VMEM((tile_side, hidden), jnp.bfloat16),
            pltpu.VMEM((tile_side, hidden), jnp.bfloat16),
            pltpu.VMEM((tile_side, hidden), jnp.bfloat16),
            pltpu.VMEM((hidden, hidden), jnp.bfloat16),
            pltpu.VMEM((near, slots, depth, tile_side), jnp.int32),
            pltpu.VMEM((packed, LANES), jnp.float32),
            pltpu.VMEM((packed, LANES), jnp.bfloat16),
            pltpu.VMEM((packed, LANES), jnp.bfloat16),
            pltpu.VMEM((groups, piece, LANES), jnp.float32),
            pltpu.VMEM((packed, LANES), jnp.bfloat16),
            pltpu.VMEM((near * tile_side, hidden), jnp.bfloat16),
            pltpu.VMEM((replicas * tile_side, near * tile_side), jnp.bfloat16),
            pltpu.VMEM((replicas * tile_side, hidden), jnp.float32),
            pltpu.VMEM((others * tile_side, hidden), jnp.float32),
            pltpu.VMEM((others * tile_side, hidden), jnp.float32),
            pltpu.SemaphoreType.DMA((4 + near,)),
            pltpu.SemaphoreType.DMA((2,)),
            pltpu.SemaphoreType.DMA((2, groups)),
            pltpu.SemaphoreType.DMA((2,)),
            pltpu.SemaphoreType.DMA((near,)),
            pltpu.SemaphoreType.DMA((near,)),
            pltpu.SemaphoreType.DMA((others,)),
            pltpu.SemaphoreType.DMA((others,)),
        ],
        compiler_params=pltpu.CompilerParams(
            collective_id=0, has_side_effects=True, vmem_limit_bytes=32 * 1024 * 1024
        ),
    )(
        held(grad_out),
        held(preact),
        held(aggregated),
        held(weight),
        held(degree.reshape(1, tile_side)),
        held(neighbors),
        held(jnp.swapaxes(tile_col, 2, 3)),
        held(tile_count),
    )


def solution(mesh):
    return jax.shard_map(
        functools.partial(on_device, mesh.shape["blk"], mesh.shape["rep"]),
        mesh=mesh,
        in_specs=(
            P(("blk", "rep"), None),
            P(("blk", "rep"), None),
            P(("blk", "rep"), None),
            P(),
            P(("blk", "rep")),
            P("blk", "rep", None, None, None, None),
            P("blk", "rep", None, None),
            P("blk", "rep", None),
        ),
        out_specs=(P(("blk", "rep"), None), P()),
        check_vma=False,
    )
```

```python
import functools

import jax
import jax.numpy as jnp
from jax import lax
from jax.experimental import pallas as pl
from jax.experimental.pallas import tpu as pltpu
from jax.sharding import PartitionSpec as P

MESH = pl.DeviceIdType.MESH
REACH = 2
LANES = 128
PACKED_ROWS = 16


def kernel(
    blocks,
    replicas,
    members,
    offsets,
    grad_out_hbm,
    preact_hbm,
    aggregated_hbm,
    weight_hbm,
    degree_ref,
    neighbors_hbm,
    column_ref,
    count_ref,
    features_ref,
    raw_ref,
    grad_out_ref,
    preact_ref,
    aggregated_ref,
    weight_ref,
    listed_ref,
    local_ref,
    part_ref,
    spread_ref,
    across_ref,
    gathered_ref,
    rows_ref,
    tiles_ref,
    begun_ref,
    partial_ref,
    landed_ref,
    load_sem,
    spread_sem,
    across_sem,
    gather_sem,
    rows_send_sem,
    rows_recv_sem,
    partial_send_sem,
    partial_recv_sem,
):
    block, replica = lax.axis_index("blk"), lax.axis_index("rep")
    side = members // replicas
    groups = blocks // side
    group, place = block // side, lax.rem(block, side)
    member = place * replicas + replica
    tile_side, hidden = grad_out_ref.shape
    slots = listed_ref.shape[1]
    depth = listed_ref.shape[2]
    piece = part_ref.shape[0] // members
    halves = hidden // LANES

    def across_device(step):
        return (lax.rem(group + step, groups) * side + place, replica)

    def each_member(act):
        def at_distance(step, carry):
            peer_place = lax.rem(place + step, side)
            for other in range(replicas):
                act(
                    (group * side + peer_place, other),
                    peer_place * replicas + other,
                    (step - 1) * replicas + replica,
                )
            return carry

        lax.fori_loop(1, side, at_distance, 0)
        for step in range(1, replicas):
            other = lax.rem(replica + step, replicas)
            act((block, other), place * replicas + other, (side - 1) * replicas + step - 1)

    def near_device(offset):
        return (lax.rem(block + offset + blocks, blocks), replica)

    def replica_device(step):
        return (block, lax.rem(replica + step, replicas))

    def piece_rows(index):
        return pl.ds(pl.multiple_of(index * piece, piece), piece)

    loads = [
        pltpu.make_async_copy(source, target, load_sem.at[index])
        for index, (source, target) in enumerate(
            (
                (grad_out_hbm, grad_out_ref),
                (preact_hbm, preact_ref),
                (aggregated_hbm, aggregated_ref),
                (weight_hbm, weight_ref),
            )
        )
    ]
    sources = [block] + [lax.rem(block - offset + blocks, blocks) for offset in offsets]
    for index, source in enumerate(sources):
        loads.append(
            pltpu.make_async_copy(
                neighbors_hbm.at[0, 0, source], listed_ref.at[index], load_sem.at[4 + index]
            )
        )
    for load in loads:
        load.start()

    barrier = pltpu.get_barrier_semaphore()

    def greet(target):
        pl.semaphore_signal(barrier, inc=1, device_id=target, device_id_type=MESH)

    each_member(lambda target, index, slot: greet(target))
    greeted = members - 1
    if groups > 1:
        for step in range(1, groups):
            greet(across_device(step))
        for offset in offsets:
            greet(near_device(offset))
        for step in range(1, replicas):
            greet(replica_device(step))
        greeted += groups - 1 + len(offsets) + replicas - 1

    inverse = 1.0 / jnp.sqrt(degree_ref[...].astype(jnp.float32))
    inverse = jnp.transpose(jnp.broadcast_to(inverse, (tile_side, tile_side)))[:, :1]

    loads[0].wait()
    loads[1].wait()
    loads[2].wait()
    grad_pre = jnp.where(
        preact_ref[...].astype(jnp.float32) > 0, grad_out_ref[...].astype(jnp.float32), 0.0
    ).astype(jnp.bfloat16)
    local = lax.dot_general(
        aggregated_ref[...], grad_pre, (((0,), (0,)), ((), ())), preferred_element_type=jnp.float32
    )
    for half in range(halves):
        rows = pl.ds(half * hidden, hidden)
        columns = local[:, half * LANES : (half + 1) * LANES]
        local_ref[rows] = columns
        part_ref[rows] = columns.astype(jnp.bfloat16)
    pl.semaphore_wait(barrier, greeted)

    def send_piece(target, index, slot):
        pltpu.make_async_remote_copy(
            src_ref=part_ref.at[piece_rows(index)],
            dst_ref=spread_ref.at[piece_rows(slot)],
            send_sem=spread_sem.at[0],
            recv_sem=spread_sem.at[1],
            device_id=target,
            device_id_type=MESH,
        ).start()

    each_member(send_piece)

    loads[3].wait()
    backward = lax.dot_general(
        grad_pre, weight_ref[...], (((1,), (1,)), ((), ())), preferred_element_type=jnp.float32
    )
    rows_ref[pl.ds(0, tile_side)] = (backward * inverse).astype(jnp.bfloat16)

    row_copies = []
    for index, offset in enumerate(offsets):
        copy = pltpu.make_async_remote_copy(
            src_ref=rows_ref.at[pl.ds(0, tile_side)],
            dst_ref=rows_ref.at[pl.ds((index + 1) * tile_side, tile_side)],
            send_sem=rows_send_sem.at[index],
            recv_sem=rows_recv_sem.at[index],
            device_id=near_device(offset),
            device_id_type=MESH,
        )
        copy.start()
        row_copies.append(copy)

    chunk = tile_side // 2
    positions = lax.broadcasted_iota(jnp.int32, (chunk, tile_side), 0)
    for load in loads[4:]:
        load.wait()

    def build_tiles(index, carry):
        source = sources[0]
        for other in range(1, len(sources)):
            source = jnp.where(index == other, sources[other], source)
        lanes = pl.ds(pl.multiple_of(index * tile_side, tile_side), tile_side)
        weights = []
        for slot in range(slots):
            column = column_ref[0, 0, slot, source]
            present = slot < count_ref[0, 0, source]
            weights.append([
                jnp.where(
                    jnp.logical_and(present, column == lax.rem(replica + step, replicas)), 1.0, 0.0
                )
                for step in range(replicas)
            ])
        for start in range(0, tile_side, chunk):
            totals = [None] * replicas
            for slot in range(slots):
                counted = jnp.zeros((chunk, tile_side), jnp.float32)
                for entry in range(depth):
                    listed = listed_ref[index, slot, pl.ds(entry, 1), :] - start
                    counted += jnp.where(listed == positions, 1.0, 0.0)
                for step in range(replicas):
                    term = counted * weights[slot][step]
                    totals[step] = term if slot == 0 else totals[step] + term
            for step in range(replicas):
                tiles_ref[pl.ds(step * tile_side + start, chunk), lanes] = totals[step].astype(
                    jnp.bfloat16
                )
        return carry

    lax.fori_loop(0, 2, build_tiles, 0)

    def product(first_row, row_count, first_source, source_count):
        return jnp.dot(
            tiles_ref[
                pl.ds(first_row * tile_side, row_count * tile_side),
                pl.ds(first_source * tile_side, source_count * tile_side),
            ],
            rows_ref[pl.ds(first_source * tile_side, source_count * tile_side)],
            preferred_element_type=jnp.float32,
        )

    def wait_all(ref, sem, count):
        rows = ref.at[pl.ds(0, count * piece)]
        pltpu.make_async_copy(rows, rows, sem).wait()

    wait_all(spread_ref, spread_sem.at[1], members - 1)
    reduced = local_ref[piece_rows(member)]
    for step in range(members - 1):
        reduced += spread_ref[pl.ds(step * piece, piece)].astype(jnp.float32)

    if groups > 1:
        across_ref[0] = reduced
        across_copies = []
        for step in range(1, groups):
            copy = pltpu.make_async_remote_copy(
                src_ref=across_ref.at[0],
                dst_ref=across_ref.at[step],
                send_sem=across_sem.at[0, step],
                recv_sem=across_sem.at[1, step],
                device_id=across_device(step),
                device_id_type=MESH,
            )
            copy.start()
            across_copies.append(copy)
        for step in range(1, groups):
            across_copies[step - 1].wait()
            reduced += across_ref[step]

    gathered_ref[piece_rows(member)] = reduced.astype(jnp.bfloat16)

    def send_reduced(target, index, slot):
        pltpu.make_async_remote_copy(
            src_ref=gathered_ref.at[piece_rows(member)],
            dst_ref=gathered_ref.at[piece_rows(member)],
            send_sem=gather_sem.at[0],
            recv_sem=gather_sem.at[1],
            device_id=target,
            device_id_type=MESH,
        ).start()

    each_member(send_reduced)
    lax.fori_loop(2, len(sources), build_tiles, 0)

    early = len(sources) // 2 + 1
    for copy in row_copies[: early - 1]:
        copy.wait_recv()
    begun_ref[...] = product(0, replicas, 0, early)
    for copy in row_copies[early - 1 :]:
        copy.wait_recv()
    partial_copies = []
    if replicas > 1:
        others = pl.ds(tile_side, (replicas - 1) * tile_side)
        partial_ref[...] = begun_ref[others] + product(
            1, replicas - 1, early, len(sources) - early
        )
        for step in range(1, replicas):
            copy = pltpu.make_async_remote_copy(
                src_ref=partial_ref.at[pl.ds((step - 1) * tile_side, tile_side)],
                dst_ref=landed_ref.at[pl.ds((step - 1) * tile_side, tile_side)],
                send_sem=partial_send_sem.at[step - 1],
                recv_sem=partial_recv_sem.at[step - 1],
                device_id=replica_device(step),
                device_id_type=MESH,
            )
            copy.start()
            partial_copies.append(copy)
    owned = begun_ref[pl.ds(0, tile_side)] + product(0, 1, early, len(sources) - early)
    for step, copy in enumerate(partial_copies):
        copy.wait_recv()
        owned += landed_ref[pl.ds(step * tile_side, tile_side)]
    features_ref[...] = (owned * inverse).astype(jnp.bfloat16)

    wait_all(gathered_ref, gather_sem.at[1], members - 1)
    raw_ref[...] = gathered_ref[...]

    wait_all(spread_ref, spread_sem.at[0], members - 1)
    wait_all(gathered_ref, gather_sem.at[0], members - 1)
    for copy in row_copies + partial_copies:
        copy.wait_send()


def finish(features_ref, raw_ref, features_hbm, weight_hbm, weight_ref, sem):
    features_copy = pltpu.make_async_copy(features_ref, features_hbm, sem.at[0])
    features_copy.start()
    hidden = weight_ref.shape[0]
    raw = raw_ref[...].astype(jnp.float32)
    total = jnp.sum(jnp.sum(raw * raw, axis=0, keepdims=True), axis=1, keepdims=True)
    scale = jnp.minimum(1.0, 128.0 / jnp.sqrt(total + 1e-06))
    for half in range(hidden // LANES):
        weight_ref[:, pl.ds(half * LANES, LANES)] = (
            raw[half * hidden : (half + 1) * hidden] * scale
        )
    weight_copy = pltpu.make_async_copy(weight_ref, weight_hbm, sem.at[1])
    weight_copy.start()
    features_copy.wait()
    weight_copy.wait()


def on_device(
    blocks, replicas, grad_out, preact, aggregated, weight, degree, neighbors, tile_col, tile_count
):
    tile_side, hidden = grad_out.shape
    slots, depth = neighbors.shape[3], neighbors.shape[4]
    packed = hidden * hidden // LANES
    members = min(blocks * replicas, packed // PACKED_ROWS)
    groups = blocks * replicas // members
    piece = packed // members
    offsets = []
    for distance in range(REACH, 0, -1):
        for offset in (distance, -distance):
            if offset % blocks and offset % blocks not in [o % blocks for o in offsets]:
                offsets.append(offset)
    near = len(offsets) + 1
    others = max(replicas - 1, 1)
    held = functools.partial(pltpu.with_memory_space_constraint, memory_space=pltpu.HBM)
    hbm = pl.BlockSpec(memory_space=pltpu.HBM)
    vmem = pl.BlockSpec(memory_space=pltpu.VMEM)
    smem = pl.BlockSpec(memory_space=pltpu.SMEM)
    features, raw = pl.pallas_call(
        functools.partial(kernel, blocks, replicas, members, tuple(offsets)),
        out_shape=(
            pltpu.VMEM((tile_side, hidden), jnp.bfloat16),
            pltpu.VMEM((packed, LANES), jnp.bfloat16),
        ),
        in_specs=[hbm, hbm, hbm, hbm, vmem, hbm, smem, smem],
        out_specs=(vmem, vmem),
        scratch_shapes=[
            pltpu.VMEM((tile_side, hidden), jnp.bfloat16),
            pltpu.VMEM((tile_side, hidden), jnp.bfloat16),
            pltpu.VMEM((tile_side, hidden), jnp.bfloat16),
            pltpu.VMEM((hidden, hidden), jnp.bfloat16),
            pltpu.VMEM((near, slots, depth, tile_side), jnp.int32),
            pltpu.VMEM((packed, LANES), jnp.float32),
            pltpu.VMEM((packed, LANES), jnp.bfloat16),
            pltpu.VMEM((packed, LANES), jnp.bfloat16),
            pltpu.VMEM((groups, piece, LANES), jnp.float32),
            pltpu.VMEM((packed, LANES), jnp.bfloat16),
            pltpu.VMEM((near * tile_side, hidden), jnp.bfloat16),
            pltpu.VMEM((replicas * tile_side, near * tile_side), jnp.bfloat16),
            pltpu.VMEM((replicas * tile_side, hidden), jnp.float32),
            pltpu.VMEM((others * tile_side, hidden), jnp.float32),
            pltpu.VMEM((others * tile_side, hidden), jnp.float32),
            pltpu.SemaphoreType.DMA((4 + near,)),
            pltpu.SemaphoreType.DMA((2,)),
            pltpu.SemaphoreType.DMA((2, groups)),
            pltpu.SemaphoreType.DMA((2,)),
            pltpu.SemaphoreType.DMA((near,)),
            pltpu.SemaphoreType.DMA((near,)),
            pltpu.SemaphoreType.DMA((others,)),
            pltpu.SemaphoreType.DMA((others,)),
        ],
        compiler_params=pltpu.CompilerParams(
            collective_id=0, has_side_effects=True, vmem_limit_bytes=32 * 1024 * 1024
        ),
    )(
        held(grad_out),
        held(preact),
        held(aggregated),
        held(weight),
        held(degree.reshape(1, tile_side)),
        held(neighbors),
        held(jnp.swapaxes(tile_col, 2, 3)),
        held(tile_count),
    )
    return pl.pallas_call(
        finish,
        out_shape=(
            jax.ShapeDtypeStruct((tile_side, hidden), jnp.bfloat16),
            jax.ShapeDtypeStruct((hidden, hidden), jnp.float32),
        ),
        in_specs=[vmem, vmem],
        out_specs=(hbm, hbm),
        scratch_shapes=[
            pltpu.VMEM((hidden, hidden), jnp.float32),
            pltpu.SemaphoreType.DMA((2,)),
        ],
    )(features, raw)


def solution(mesh):
    return jax.shard_map(
        functools.partial(on_device, mesh.shape["blk"], mesh.shape["rep"]),
        mesh=mesh,
        in_specs=(
            P(("blk", "rep"), None),
            P(("blk", "rep"), None),
            P(("blk", "rep"), None),
            P(),
            P(("blk", "rep")),
            P("blk", "rep", None, None, None, None),
            P("blk", "rep", None, None),
            P("blk", "rep", None),
        ),
        out_specs=(P(("blk", "rep"), None), P()),
        check_vma=False,
    )
```
